256 devices in a mesh: dev: 256 (over x, z, y, core).
Axes of the slice: x: 4, y: 4, z: 8, core: 2. Of those that a mesh axis runs over, the one named last changes fastest.
Arguments:
- state: float32 [5, 64, 131072], P(None, None, 'dev'), as said below
- step_size: float32 [1], replicated, may hold values from 0.0003 to 0.0006
- levels: int32 [131072], P('dev'), may hold values from 6 to 7, as said below
- send_faces: int32 [2048, 128], P('dev'), may hold values from 0 to 3072, as said below
- partner: int32 [6, 131072], P(None, 'dev'), may hold values from 0 to 4096, as said below
- mortar_in: int32 [5, 10240], P(None, 'dev'), may hold values from 0 to 4096, as said below
- mortar_dir: int32 [10240], P('dev'), may hold values from 0 to 3, as said below
- return_faces: int32 [512, 32], P('dev'), may hold values from 0 to 200, as said below
- flux_source: int32 [6, 131072], P(None, 'dev'), may hold values from 0 to 264, as said below
Outputs:
- increment: float32 [5, 64, 131072], P(None, None, 'dev')
The draws below stay inside these ranges and needn't reach their ends.
Inputs may be any that keep to these rules, and one draw needn't show every extreme that they name: At every node the entries are density, momenta and total energy of a state with density from 1 to 1.5, velocity components from -0.2 to 0.2 and pressure from 1 to 1.5. `levels`: every element has level 6 or 7. `send_faces`: row 8 d + p lists local face numbers of device d whose traces its peer p needs; 3072 marks an empty entry. Faces are either conforming (opposite faces of two elements of one level, each the other's partner) or hanging (one face and four faces of elements one level finer meet in exactly one mortar); partners lie within 4 devices along the curve, mortars join faces of one device or of two adjacent ones. Hanging faces have partner 6 * 512. `mortar_in`: unused mortar entries name 3072 in all five rows. `mortar_dir`: unused mortar entries have 0. `return_faces`: 200 marks an empty entry. `flux_source`: 200 exactly for conforming faces.
All inputs are finite; a program needn't handle non-finite values.
Results may differ from the reference program's by a relative error of at most 0.0003.
Values sent between devices are 32-bit elements; how exact they have to be, the bound alone decides.
A program may use at most 64 MiB of HBM per device.

```python
import math
import jax
import jax.numpy as jnp
import numpy as np
from jax import lax

ELEM_DEV = 512
ELEMS = 131072
HOP = 4
PEERS = 8
SLOTS = 128
CROSS_HANG = 8
RETURN_SLOTS = 32
MORTAR_SLOTS = 40
LEVEL = 6
N_DEV = 256


def device_random(key, device):
    fine_least = ELEM_DEV // 128
    fine_most = 3 * ELEM_DEV // 64
    forced = jax.random.randint(jax.random.fold_in(key, 101), (2,), 0, N_DEV)
    own_key = jax.random.fold_in(jax.random.fold_in(key, 102), device)
    groups = jax.random.randint(jax.random.fold_in(own_key, 1), (), fine_least, fine_most + 1)
    groups = jnp.where(device == forced[1], fine_most, groups)
    ranking = jax.random.permutation(jax.random.fold_in(own_key, 2), ELEM_DEV // 8)
    fine = jnp.repeat((ranking < groups).astype(jnp.int32), 8)
    orders = []
    for face in range(6):
        shuffle = jax.random.permutation(jax.random.fold_in(own_key, 3 + face), ELEM_DEV)
        orders.append(jnp.argsort(fine * ELEM_DEV + shuffle, stable=True).astype(jnp.int32))
    places = [jax.random.permutation(jax.random.fold_in(own_key, 10 + peer), SLOTS).astype(jnp.int32) for peer in range(PEERS)]
    backs = [jax.random.permutation(jax.random.fold_in(own_key, 40 + side), RETURN_SLOTS).astype(jnp.int32) for side in range(2)]
    mortar_places = jax.random.permutation(jax.random.fold_in(own_key, 50), MORTAR_SLOTS).astype(jnp.int32)
    owner_bit = jax.random.randint(jax.random.fold_in(own_key, 51), (), 0, 2)
    owner_bit = jnp.where(device == forced[0], 1, jnp.where(device == (forced[0] + 1) % N_DEV, 0, owner_bit))
    return {'groups': groups, 'fine': fine, 'orders': orders, 'places': places, 'backs': backs, 'mortar_places': mortar_places, 'owner_bit': owner_bit}


def build_device(key, device):
    here = device_random(key, device)
    beside_all = {}
    for offset in range(1, HOP + 1):
        beside_all[offset] = device_random(key, (device + offset) % N_DEV)
        beside_all[-offset] = device_random(key, (device - offset) % N_DEV)
    width = ELEM_DEV
    empty_trace = 6 * width
    base = empty_trace + 1
    empty_flux = 5 * MORTAR_SLOTS
    return_base = empty_flux + 1
    hang = CROSS_HANG
    first_cut = SLOTS - 4 * hang
    big_start = first_cut + SLOTS
    coarse_count = width - 8 * here['groups']
    local_pairs = here['groups'] // 2
    bit_here = here['owner_bit']
    bit_before = beside_all[-1]['owner_bit']
    orders = here['orders']

    def take(table, index, limit):
        return table[jnp.clip(index, 0, limit - 1)]

    def received(peer_offset, index):
        peer = peer_offset - 1 if peer_offset > 0 else HOP - peer_offset - 1
        return base + peer * SLOTS + take(beside_all[-peer_offset]['places'][peer], index, SLOTS)

    def returned(side, index):
        sender = beside_all[-1] if side == 0 else beside_all[1]
        return return_base + side * RETURN_SLOTS + take(sender['backs'][side], index, RETURN_SLOTS)

    def mortar_slot(index):
        return take(here['mortar_places'], index, MORTAR_SLOTS)
    rank = jnp.arange(width, dtype=jnp.int32)
    fine_rank = rank - coarse_count
    fine_pos = jnp.clip(fine_rank, 0, width - 1)
    defaults = [(face ^ 1) * width + orders[face ^ 1][rank] for face in range(6)]
    coarse_hang = rank < local_pairs
    fine_hang = (fine_rank >= 0) & (fine_rank < 4 * local_pairs)
    quarter_flux = (1 + fine_pos % 4) * MORTAR_SLOTS
    partner_zero = jnp.where(coarse_hang | fine_hang, empty_trace, defaults[0])
    flux_zero = jnp.where(coarse_hang, mortar_slot(local_pairs + rank), jnp.where(fine_hang, quarter_flux + mortar_slot(fine_pos // 4), empty_flux))
    partner_one = jnp.where(coarse_hang | fine_hang, empty_trace, defaults[1])
    flux_one = jnp.where(coarse_hang, mortar_slot(rank), jnp.where(fine_hang, quarter_flux + mortar_slot(local_pairs + fine_pos // 4), empty_flux))
    nearest = rank < first_cut
    second = (rank >= first_cut) & (rank < big_start)
    bigs = (rank >= big_start) & (rank < big_start + hang)
    smalls = (fine_rank >= 0) & (fine_rank < 4 * hang)
    big_index = rank - big_start
    partner_two = jnp.where(nearest, received(1, rank), jnp.where(second, received(2, rank - first_cut), jnp.where(bigs | smalls, empty_trace, defaults[2])))
    flux_two = jnp.where(bigs, jnp.where(bit_before == 1, mortar_slot(2 * local_pairs + hang + big_index), returned(0, big_index)), jnp.where(smalls, jnp.where(bit_before == 1, returned(0, fine_pos), quarter_flux + mortar_slot(2 * local_pairs + hang + fine_pos // 4)), empty_flux))
    partner_three = jnp.where(nearest, received(-1, rank), jnp.where(second, received(-2, rank - first_cut), jnp.where(bigs | smalls, empty_trace, defaults[3])))
    flux_three = jnp.where(bigs, jnp.where(bit_here == 1, mortar_slot(2 * local_pairs + big_index), returned(1, big_index)), jnp.where(smalls, jnp.where(bit_here == 1, returned(1, fine_pos), quarter_flux + mortar_slot(2 * local_pairs + fine_pos // 4)), empty_flux))
    partner_four = jnp.where(rank < SLOTS, received(3, rank), jnp.where(rank < 2 * SLOTS, received(4, rank - SLOTS), defaults[4]))
    partner_five = jnp.where(rank < SLOTS, received(-3, rank), jnp.where(rank < 2 * SLOTS, received(-4, rank - SLOTS), defaults[5]))
    conform_flux = jnp.full((width,), empty_flux, jnp.int32)
    by_rank = [partner_zero, partner_one, partner_two, partner_three, partner_four, partner_five]
    flux_rank = [flux_zero, flux_one, flux_two, flux_three, conform_flux, conform_flux]
    partner = jnp.stack([jnp.zeros((width,), jnp.int32).at[orders[face]].set(by_rank[face].astype(jnp.int32)) for face in range(6)])
    sources = jnp.stack([jnp.zeros((width,), jnp.int32).at[orders[face]].set(flux_rank[face].astype(jnp.int32)) for face in range(6)])
    slot = jnp.arange(SLOTS, dtype=jnp.int32)
    extra = slot - first_cut
    plus_y = orders[3]
    minus_y = orders[2]
    forward_one = jnp.where(slot < first_cut, 3 * width + take(plus_y, slot, width), jnp.where(bit_here == 1, jnp.where(extra < 4 * hang, 3 * width + take(plus_y, coarse_count + extra, width), empty_trace), jnp.where(extra < hang, 3 * width + take(plus_y, big_start + extra, width), empty_trace)))
    backward_one = jnp.where(slot < first_cut, 2 * width + take(minus_y, slot, width), jnp.where(bit_before == 1, jnp.where(extra < 4 * hang, 2 * width + take(minus_y, coarse_count + extra, width), empty_trace), jnp.where(extra < hang, 2 * width + take(minus_y, big_start + extra, width), empty_trace)))
    lists = [forward_one, 3 * width + take(plus_y, first_cut + slot, width), 5 * width + take(orders[5], slot, width), 5 * width + take(orders[5], SLOTS + slot, width), backward_one, 2 * width + take(minus_y, first_cut + slot, width), 4 * width + take(orders[4], slot, width), 4 * width + take(orders[4], SLOTS + slot, width)]
    sends = jnp.stack([jnp.full((SLOTS,), empty_trace, jnp.int32).at[here['places'][peer]].set(lists[peer].astype(jnp.int32)) for peer in range(PEERS)])
    entry = jnp.arange(MORTAR_SLOTS, dtype=jnp.int32)
    in_local_a = entry < local_pairs
    in_local_b = (entry >= local_pairs) & (entry < 2 * local_pairs)
    in_after = (entry >= 2 * local_pairs) & (entry < 2 * local_pairs + hang)
    in_before = (entry >= 2 * local_pairs + hang) & (entry < 2 * local_pairs + 2 * hang)
    index_b = entry - local_pairs
    index_after = entry - 2 * local_pairs
    index_before = entry - 2 * local_pairs - hang
    big = jnp.where(in_local_a, width + take(orders[1], entry, width), jnp.where(in_local_b, take(orders[0], index_b, width), jnp.where(in_after, jnp.where(bit_here == 1, 3 * width + take(plus_y, big_start + index_after, width), received(-1, first_cut + index_after)), jnp.where(in_before, jnp.where(bit_before == 1, 2 * width + take(minus_y, big_start + index_before, width), received(1, first_cut + index_before)), empty_trace))))

    def small(quarter):
        return jnp.where(in_local_a, take(orders[0], coarse_count + 4 * entry + quarter, width), jnp.where(in_local_b, width + take(orders[1], coarse_count + 4 * index_b + quarter, width), jnp.where(in_after, jnp.where(bit_here == 1, received(-1, first_cut + 4 * index_after + quarter), 3 * width + take(plus_y, coarse_count + 4 * index_after + quarter, width)), jnp.where(in_before, jnp.where(bit_before == 1, received(1, first_cut + 4 * index_before + quarter), 2 * width + take(minus_y, coarse_count + 4 * index_before + quarter, width)), empty_trace))))
    direction = jnp.where(in_local_a, 1, jnp.where(in_local_b, 0, jnp.where(in_after, jnp.where(bit_here == 1, 3, 2), jnp.where(in_before, jnp.where(bit_before == 1, 2, 3), 0))))
    entries = jnp.stack([big] + [small(quarter) for quarter in range(4)]).astype(jnp.int32)
    mortar_in = jnp.zeros((5, MORTAR_SLOTS), jnp.int32).at[:, here['mortar_places']].set(entries)
    mortar_dir = jnp.zeros((MORTAR_SLOTS,), jnp.int32).at[here['mortar_places']].set(direction.astype(jnp.int32))
    back_slot = jnp.arange(RETURN_SLOTS, dtype=jnp.int32)
    quarter_of = (1 + back_slot % 4) * MORTAR_SLOTS
    pair_of = back_slot // 4
    to_after = jnp.where(bit_here == 1, quarter_of + mortar_slot(2 * local_pairs + pair_of), jnp.where(back_slot < hang, mortar_slot(2 * local_pairs + back_slot), empty_flux))
    to_before = jnp.where(bit_before == 1, quarter_of + mortar_slot(2 * local_pairs + hang + pair_of), jnp.where(back_slot < hang, mortar_slot(2 * local_pairs + hang + back_slot), empty_flux))
    back_lists = [to_after, to_before]
    returns = jnp.stack([jnp.full((RETURN_SLOTS,), empty_flux, jnp.int32).at[here['backs'][side]].set(back_lists[side].astype(jnp.int32)) for side in range(2)])
    levels = (LEVEL + here['fine']).astype(jnp.int32)
    return (levels, sends, partner, mortar_in, mortar_dir, returns, sources)


def mesh_part(key, which):
    devices = jnp.arange(N_DEV, dtype=jnp.int32)
    built = jax.vmap(build_device, in_axes=(None, 0))(jax.random.fold_in(key, 7), devices)
    return built[which]


def draw_levels(key, part):
    return mesh_part(key, 0).reshape(ELEMS)


def draw_send_faces(key, part):
    return mesh_part(key, 1).reshape(N_DEV * PEERS, SLOTS)


def draw_partner(key, part):
    return jnp.transpose(mesh_part(key, 2), (1, 0, 2)).reshape(6, ELEMS)


def draw_mortar_in(key, part):
    return jnp.transpose(mesh_part(key, 3), (1, 0, 2)).reshape(5, N_DEV * MORTAR_SLOTS)


def draw_mortar_dir(key, part):
    return mesh_part(key, 4).reshape(N_DEV * MORTAR_SLOTS)


def draw_return_faces(key, part):
    return mesh_part(key, 5).reshape(2 * N_DEV, RETURN_SLOTS)


def draw_flux_source(key, part):
    return jnp.transpose(mesh_part(key, 6), (1, 0, 2)).reshape(6, ELEMS)


def draw_state(key, part):
    keys = jax.random.split(key, 3)
    shape = (64, ELEMS)
    density = jax.random.uniform(keys[0], shape, minval=1.0, maxval=1.5)
    motion = jax.random.uniform(keys[1], (3,) + shape, minval=-0.2, maxval=0.2)
    pressure = jax.random.uniform(keys[2], shape, minval=1.0, maxval=1.5)
    energy = pressure / 0.4 + 0.5 * density * (motion[0] * motion[0] + motion[1] * motion[1] + motion[2] * motion[2])
    return jnp.stack([density, density * motion[0], density * motion[1], density * motion[2], energy]).astype(jnp.float32)


def level_of(stream_key, dims, cuts, least, largest):
    loudness = 1.0
    for axis_at, blocks in cuts:
        steps = jax.random.uniform(jax.random.fold_in(jax.random.fold_in(stream_key, 6), axis_at), (blocks,), jnp.float32, least / len(cuts), largest / len(cuts))
        loudness = loudness * jnp.repeat(jnp.exp(steps), dims[axis_at] // blocks).reshape((-1,) + (1,) * (len(dims) - 1 - axis_at))
    return loudness


def setup_inputs(seed: int = 0) -> dict:
    key_of = jax.random.split(jax.random.key(seed), 10)
    return {
        "state": draw_state(jax.random.fold_in(key_of[9], 71), 0),
        "step_size": jnp.clip(jnp.exp(jax.random.uniform(key_of[1], (1,), jnp.float32, math.log(0.0003), math.log(0.0006))), 0.0003, 0.0006),
        "levels": draw_levels(jax.random.fold_in(key_of[9], 71), 0),
        "send_faces": draw_send_faces(jax.random.fold_in(key_of[9], 71), 0),
        "partner": draw_partner(jax.random.fold_in(key_of[9], 71), 0),
        "mortar_in": draw_mortar_in(jax.random.fold_in(key_of[9], 71), 0),
        "mortar_dir": draw_mortar_dir(jax.random.fold_in(key_of[9], 71), 0),
        "return_faces": draw_return_faces(jax.random.fold_in(key_of[9], 71), 0),
        "flux_source": draw_flux_source(jax.random.fold_in(key_of[9], 71), 0),
    }


GAMMA = 1.4
HIGHEST = lax.Precision.HIGHEST

def lobatto_tables():
    nodes = np.array([-1.0, -1.0 / np.sqrt(5.0), 1.0 / np.sqrt(5.0), 1.0])
    weights = np.array([1.0, 5.0, 5.0, 1.0]) / 6.0

    def basis(points):
        table = np.ones((len(points), 4))
        for column in range(4):
            for other in range(4):
                if other != column:
                    table[:, column] *= (points - nodes[other]) / (nodes[column] - nodes[other])
        return table
    derivative = np.zeros((4, 4))
    for row in range(4):
        for column in range(4):
            total = 0.0
            for other in range(4):
                if other != column:
                    term = 1.0 / (nodes[column] - nodes[other])
                    for third in range(4):
                        if third != column and third != other:
                            term *= (nodes[row] - nodes[third]) / (nodes[column] - nodes[third])
                    total += term
            derivative[row, column] = total
    lower = basis((nodes - 1.0) / 2.0)
    upper = basis((nodes + 1.0) / 2.0)
    back_lower = 0.5 * (lower.T * weights[None, :]) / weights[:, None]
    back_upper = 0.5 * (upper.T * weights[None, :]) / weights[:, None]
    return [np.asarray(table, np.float32) for table in (derivative, lower, upper, back_lower, back_upper)]

def face_node_table():
    table = np.zeros((6, 16), np.int32)
    for face in range(6):
        axis = face // 2
        others = [dimension for dimension in range(3) if dimension != axis]
        count = 0
        for first in range(4):
            for second in range(4):
                spot = [0, 0, 0]
                spot[axis] = 3 * (face % 2)
                spot[others[0]] = first
                spot[others[1]] = second
                table[face, count] = 16 * spot[0] + 4 * spot[1] + spot[2]
                count += 1
    return table

def face_normals(count):
    signs = np.zeros((3, 6), np.float32)
    for face in range(6):
        signs[face // 2, face] = 2.0 * (face % 2) - 1.0
    return tuple((jnp.asarray(np.repeat(signs[axis], count)) for axis in range(3)))

def reference_state(count):
    values = jnp.array([1.0, 0.0, 0.0, 0.0, 2.5], jnp.float32)
    return jnp.broadcast_to(values[:, None, None], (5, 16, count))

def normal_flux(state, normal):
    density = state[0]
    motion = [state[1 + axis] / density for axis in range(3)]
    pressure = (GAMMA - 1.0) * (state[4] - 0.5 * (state[1] * motion[0] + state[2] * motion[1] + state[3] * motion[2]))
    along = motion[0] * normal[0] + motion[1] * normal[1] + motion[2] * normal[2]
    flux = jnp.stack([state[0] * along, state[1] * along + pressure * normal[0], state[2] * along + pressure * normal[1], state[3] * along + pressure * normal[2], (state[4] + pressure) * along])
    speed = jnp.abs(along) + jnp.sqrt(GAMMA * pressure / density)
    return (flux, speed)

def rusanov(inside, inside_flux, inside_speed, outside, normal):
    outside_flux, outside_speed = normal_flux(outside, normal)
    return 0.5 * (inside_flux + outside_flux) - 0.5 * jnp.maximum(inside_speed, outside_speed) * (outside - inside)

def face_traces(block):
    cube = block.reshape(5, 4, 4, 4, block.shape[-1])
    faces = [cube[:, 0], cube[:, 3], cube[:, :, 0], cube[:, :, 3], cube[:, :, :, 0], cube[:, :, :, 3]]
    return jnp.concatenate([face.reshape(5, 16, block.shape[-1]) for face in faces], axis=2)

def volume_term(block, scale):
    cube = block.reshape(5, 4, 4, 4, block.shape[-1])
    derivative = jnp.asarray(lobatto_tables()[0])
    first, _ = normal_flux(cube, (1.0, 0.0, 0.0))
    second, _ = normal_flux(cube, (0.0, 1.0, 0.0))
    third, _ = normal_flux(cube, (0.0, 0.0, 1.0))
    total = jnp.einsum('ai,vijke->vajke', derivative, first, precision=HIGHEST)
    total = total + jnp.einsum('bj,vijke->vibke', derivative, second, precision=HIGHEST)
    total = total + jnp.einsum('ck,vijke->vijce', derivative, third, precision=HIGHEST)
    return -scale * total

def add_lift(residual, jump, scale):
    count = residual.shape[-1]
    parts = -6.0 * scale * jump.reshape(5, 4, 4, 6, count)
    residual = residual.at[:, 0].add(parts[:, :, :, 0])
    residual = residual.at[:, 3].add(parts[:, :, :, 1])
    residual = residual.at[:, :, 0].add(parts[:, :, :, 2])
    residual = residual.at[:, :, 3].add(parts[:, :, :, 3])
    residual = residual.at[:, :, :, 0].add(parts[:, :, :, 4])
    residual = residual.at[:, :, :, 3].add(parts[:, :, :, 5])
    return residual

def mortar_fluxes(big, smalls, direction):
    tables = lobatto_tables()
    forward = (jnp.asarray(tables[1]), jnp.asarray(tables[2]))
    backward = (jnp.asarray(tables[3]), jnp.asarray(tables[4]))
    count = big.shape[-1]
    normal = tuple(((direction == 2 * axis + 1).astype(jnp.float32) - (direction == 2 * axis).astype(jnp.float32) for axis in range(3)))
    square = big.reshape(5, 4, 4, count)
    gathered = jnp.zeros_like(big)
    pieces = []
    for quarter in range(4):
        near = jnp.einsum('ai,bj,vijm->vabm', forward[quarter % 2], forward[quarter // 2], square, precision=HIGHEST).reshape(5, 16, count)
        near_flux, near_speed = normal_flux(near, normal)
        star = rusanov(near, near_flux, near_speed, smalls[quarter], normal)
        pieces.append(-star)
        gathered = gathered + jnp.einsum('ai,bj,vijm->vabm', backward[quarter % 2], backward[quarter // 2], star.reshape(5, 4, 4, count), precision=HIGHEST).reshape(5, 16, count)
    return jnp.concatenate([gathered] + pieces, axis=2)

def reference(state, step_size, levels, send_faces, partner, mortar_in, mortar_dir, return_faces, flux_source):
    offsets = jnp.concatenate([jnp.arange(1, HOP + 1, dtype=jnp.int32), -jnp.arange(1, HOP + 1, dtype=jnp.int32)]).astype(jnp.int32)
    nodes = jnp.asarray(face_node_table())
    empty_trace = 6 * ELEM_DEV
    empty_flux = 5 * MORTAR_SLOTS
    all_slots = N_DEV * MORTAR_SLOTS

    def global_trace(local, device):
        own = local // ELEM_DEV * ELEMS + device * ELEM_DEV + local % ELEM_DEV
        beyond = jnp.clip(local - empty_trace - 1, 0, PEERS * SLOTS - 1)
        peer = beyond // SLOTS
        sender = (device - offsets[peer]) % N_DEV
        sent = jnp.clip(send_faces[sender * PEERS + peer, beyond % SLOTS], 0, empty_trace - 1)
        remote = sent // ELEM_DEV * ELEMS + sender * ELEM_DEV + sent % ELEM_DEV
        return jnp.where(local < empty_trace, own, jnp.where(local == empty_trace, 6 * ELEMS, remote)).astype(jnp.int32)

    def fetch(index):
        flat = index.reshape(-1)
        face = jnp.clip(flat // ELEMS, 0, 5)
        element = flat % ELEMS
        values = jnp.transpose(state[:, nodes[face], element[:, None]], (0, 2, 1))
        return jnp.where((flat == 6 * ELEMS)[None, None, :], reference_state(flat.shape[0]), values)

    def global_flux(local, device):
        own = local // MORTAR_SLOTS * all_slots + device * MORTAR_SLOTS + local % MORTAR_SLOTS
        beyond = jnp.clip(local - empty_flux - 1, 0, 2 * RETURN_SLOTS - 1)
        side = beyond // RETURN_SLOTS
        sender = (device - 1 + 2 * side) % N_DEV
        sent = jnp.clip(return_faces[sender * 2 + side, beyond % RETURN_SLOTS], 0, empty_flux - 1)
        remote = sent // MORTAR_SLOTS * all_slots + sender * MORTAR_SLOTS + sent % MORTAR_SLOTS
        return jnp.where(local < empty_flux, own, jnp.where(local == empty_flux, 5 * all_slots, remote)).astype(jnp.int32)
    slot_device = jnp.arange(all_slots, dtype=jnp.int32) // MORTAR_SLOTS
    sources = [fetch(global_trace(mortar_in[row], slot_device)) for row in range(5)]
    mortars = mortar_fluxes(sources[0], sources[1:], mortar_dir)
    mortars = jnp.concatenate([mortars, jnp.zeros((5, 16, 1), jnp.float32)], axis=2)
    normals = face_normals(ELEM_DEV)

    def one_device(device):
        block = lax.dynamic_slice_in_dim(state, device * ELEM_DEV, ELEM_DEV, 2)
        scale = jnp.exp2(lax.dynamic_slice_in_dim(levels, device * ELEM_DEV, ELEM_DEV, 0).astype(jnp.float32) + 1.0)
        local = face_traces(block)
        local_flux, local_speed = normal_flux(local, normals)
        links = lax.dynamic_slice_in_dim(partner, device * ELEM_DEV, ELEM_DEV, 1).reshape(-1)
        outside = fetch(global_trace(links, device))
        conforming = rusanov(local, local_flux, local_speed, outside, normals)
        anchors = lax.dynamic_slice_in_dim(flux_source, device * ELEM_DEV, ELEM_DEV, 1).reshape(-1)
        from_mortar = mortars[:, :, global_flux(anchors, device)]
        star = jnp.where((anchors != empty_flux)[None, None, :], from_mortar, conforming)
        residual = add_lift(volume_term(block, scale), star - local_flux, scale)
        return step_size[0] * residual.reshape(5, 64, ELEM_DEV)
    blocks = lax.map(one_device, jnp.arange(N_DEV, dtype=jnp.int32))
    return jnp.transpose(blocks, (1, 2, 0, 3)).reshape(5, 64, ELEMS)
```

```python
import functools
import jax
import jax.numpy as jnp
import numpy as np
from jax import lax
from jax.experimental import pallas as pl
from jax.experimental.pallas import tpu as pltpu
from jax.sharding import PartitionSpec as P

GAMMA = 1.4
HIGHEST = lax.Precision.HIGHEST
MESH = pl.DeviceIdType.MESH
TILES = 4
SIDE = (0, 0, 1, 1, 2, 2)


def lobatto_tables():
    nodes = np.array([-1.0, -1.0 / np.sqrt(5.0), 1.0 / np.sqrt(5.0), 1.0])
    weights = np.array([1.0, 5.0, 5.0, 1.0]) / 6.0

    def basis(points):
        table = np.ones((len(points), 4))
        for column in range(4):
            for other in range(4):
                if other != column:
                    table[:, column] *= (points - nodes[other]) / (nodes[column] - nodes[other])
        return table

    derivative = np.zeros((4, 4))
    for row in range(4):
        for column in range(4):
            total = 0.0
            for other in range(4):
                if other != column:
                    term = 1.0 / (nodes[column] - nodes[other])
                    for third in range(4):
                        if third != column and third != other:
                            term *= (nodes[row] - nodes[third]) / (nodes[column] - nodes[third])
                    total += term
            derivative[row, column] = total
    lower = basis((nodes - 1.0) / 2.0)
    upper = basis((nodes + 1.0) / 2.0)
    back_lower = 0.5 * (lower.T * weights[None, :]) / weights[:, None]
    back_upper = 0.5 * (upper.T * weights[None, :]) / weights[:, None]
    return [
        np.asarray(table, np.float32)
        for table in (derivative, lower, upper, back_lower, back_upper)
    ]


def mortar_matrices():
    _, lower, upper, back_lower, back_upper = [t.astype(np.float64) for t in lobatto_tables()]
    ahead, back = (lower, upper), (back_lower, back_upper)
    five = np.eye(5)
    forth = [np.kron(five, np.kron(ahead[q % 2], ahead[q // 2])) for q in range(4)]
    home = [np.kron(five, np.kron(back[q % 2], back[q // 2])) for q in range(4)]
    return np.concatenate(forth + home, axis=0).astype(np.float32)


def lanes_of(tile, index):
    return jnp.take_along_axis(tile, index, axis=1, mode="promise_in_bounds")


def axis_flux(parts, axis, sign):
    density, energy = parts[0], parts[4]
    inverse = 1.0 / density
    along = sign * parts[1 + axis] * inverse
    kinetic = parts[1] * parts[1] + parts[2] * parts[2] + parts[3] * parts[3]
    pressure = (GAMMA - 1.0) * (energy - 0.5 * kinetic * inverse)
    flux = [density * along]
    for other in range(3):
        term = parts[1 + other] * along
        flux.append(term + sign * pressure if other == axis else term)
    flux.append((energy + pressure) * along)
    speed = jnp.abs(along) + jnp.sqrt(GAMMA * pressure * inverse)
    return flux, speed


def normal_flux(parts, normal):
    density, energy = parts[0], parts[4]
    motion = [parts[1 + axis] / density for axis in range(3)]
    pressure = (GAMMA - 1.0) * (
        energy - 0.5 * (parts[1] * motion[0] + parts[2] * motion[1] + parts[3] * motion[2])
    )
    along = motion[0] * normal[0] + motion[1] * normal[1] + motion[2] * normal[2]
    flux = [density * along]
    for axis in range(3):
        flux.append(parts[1 + axis] * along + pressure * normal[axis])
    flux.append((energy + pressure) * along)
    speed = jnp.abs(along) + jnp.sqrt(GAMMA * pressure / density)
    return flux, speed


def split(columns):
    return [columns[16 * v : 16 * v + 16] for v in range(5)]


def rest_state():
    row = lax.broadcasted_iota(jnp.int32, (80, 128), 0)
    return jnp.where(row < 16, 1.0, jnp.where(row >= 64, 2.5, 0.0)).astype(jnp.float32)


def kernel(
    count,
    state_hbm,
    levels_ref,
    send_ref,
    partner_ref,
    mortar_ref,
    dir_ref,
    return_ref,
    source_ref,
    matrix_ref,
    out_ref,
    st,
    tr,
    snd,
    rcv,
    acc,
    own,
    spd,
    res,
    ftmp,
    mor,
    tab,
    rsnd,
    rrcv,
    pad,
    jmp,
    load_sem,
    send_sem,
    recv_sem,
    rsend_sem,
    rrecv_sem,
):
    me = lax.axis_index("dev")
    derivative = [[float(x) for x in row] for row in lobatto_tables()[0]]

    def peer_of(p):
        offset = jnp.where(p < 4, p + 1, 3 - p)
        return lax.rem(me + offset + count, count)

    barrier = pltpu.get_barrier_semaphore()
    for p in range(8):
        pl.semaphore_signal(barrier, inc=1, device_id=(peer_of(p),), device_id_type=MESH)
    loads = [
        pltpu.make_async_copy(
            state_hbm.at[:, :, pl.ds(128 * c, 128)], st.at[c], load_sem.at[c]
        )
        for c in range(TILES)
    ]
    for load in loads:
        load.start()

    lane = lax.broadcasted_iota(jnp.int32, (8, 128), 1)
    lane1 = lane[0:1]
    rest = rest_state()

    pad[...] = jnp.full((8, 128), 3072, jnp.int32)
    pad[0:5, 0:40] = mortar_ref[...]
    pad[5:6, 0:40] = dir_ref[...]
    pad[6:8, 0:32] = return_ref[...]
    packed = pad[...]
    by40 = pltpu.roll(packed, 40, axis=1)
    by80 = pltpu.roll(packed, 80, axis=1)
    entry = [
        jnp.where(
            lane1 < 40,
            packed[0:1],
            jnp.where(lane1 < 80, by40[1:2], jnp.where(lane1 < 120, by80[2:3], 3072)),
        ),
        jnp.where(lane1 < 40, packed[3:4], jnp.where(lane1 < 80, by40[4:5], 3072)),
    ]
    direction = [
        jnp.where(lane1 < 40, packed[5:6], jnp.where(lane1 < 80, by40[5:6], by80[5:6])),
        jnp.where(lane1 < 40, packed[5:6], by40[5:6]),
    ]
    by32 = pltpu.roll(packed, 32, axis=1)
    by64 = pltpu.roll(packed, 64, axis=1)
    by96 = pltpu.roll(packed, 96, axis=1)
    leaving = jnp.where(
        lane < 32, packed, jnp.where(lane < 64, by32, jnp.where(lane < 96, by64, by96))
    )[6:8]

    def placed(index):
        moved = jnp.where(index > 3072, index - 1, index)
        tile = jnp.where(index == 3072, -1, jnp.right_shift(moved, 7))
        return tile, jnp.bitwise_and(moved, 127)

    def wide(row, rows=80):
        return jnp.broadcast_to(row, (rows, 128))

    for load in loads:
        load.wait()

    def trace_step(c, carry):
        for v in range(5):
            tr[0, c, 16 * v : 16 * v + 16] = st[c, v, 0:16]
            tr[1, c, 16 * v : 16 * v + 16] = st[c, v, 48:64]
            for i in range(4):
                tr[2, c, 16 * v + 4 * i : 16 * v + 4 * i + 4] = st[c, v, 16 * i : 16 * i + 4]
                tr[3, c, 16 * v + 4 * i : 16 * v + 4 * i + 4] = st[c, v, 16 * i + 12 : 16 * i + 16]
            tr[4, c, 16 * v : 16 * v + 16] = st[c, v, pl.ds(0, 16, 4)]
            tr[5, c, 16 * v : 16 * v + 16] = st[c, v, pl.ds(3, 16, 4)]
        return carry

    lax.fori_loop(0, TILES, trace_step, 0)

    pl.semaphore_wait(barrier, 8)

    def trace_copy(p):
        return pltpu.make_async_remote_copy(
            src_ref=snd.at[p],
            dst_ref=rcv.at[p],
            send_sem=send_sem.at[p],
            recv_sem=recv_sem.at[p],
            device_id=(peer_of(p),),
            device_id_type=MESH,
        )

    def order(k):
        return lax.rem(k, 2) * 4 + lax.rem(4 - k // 2, 4)

    def send_step(k, carry):
        p = order(k)
        index = send_ref[pl.ds(p, 1), :]
        tile = wide(jnp.right_shift(index, 7))
        place = wide(jnp.bitwise_and(index, 127))
        value = rest
        for f in range(6):
            for c in range(TILES):
                value = jnp.where(tile == f * TILES + c, lanes_of(tr[f, c], place), value)
        snd[p] = value
        trace_copy(p).start()
        return carry

    lax.fori_loop(0, 8, send_step, 0)

    for m in range(2):
        tile, place = placed(entry[m])
        tile, place = wide(tile), wide(place)
        value = rest
        for f in range(4):
            for c in range(TILES):
                value = jnp.where(tile == f * TILES + c, lanes_of(tr[f, c], place), value)
        mor[m] = value

    row16 = lax.broadcasted_iota(jnp.int32, (16, 128), 0)
    second = jnp.right_shift(row16, 2)

    def by_row(shift):
        picks = [derivative[j][(j - shift) % 4] for j in range(4)]
        return jnp.where(
            second == 0,
            picks[0],
            jnp.where(second == 1, picks[1], jnp.where(second == 2, picks[2], picks[3])),
        ).astype(jnp.float32)

    weights = [by_row(shift) for shift in range(4)]

    def volume_step(c, carry):
        for i in range(4):
            rows = pl.ds(16 * i, 16)
            parts = [st[c, v, rows] for v in range(5)]
            inverse = 1.0 / parts[0]
            motion = [parts[1 + a] * inverse for a in range(3)]
            pressure = (GAMMA - 1.0) * (
                parts[4]
                - 0.5 * (parts[1] * motion[0] + parts[2] * motion[1] + parts[3] * motion[2])
            )
            for axis in range(3):
                flux = [parts[1 + axis]]
                for other in range(3):
                    term = parts[1 + other] * motion[axis]
                    flux.append(term + pressure if other == axis else term)
                flux.append((parts[4] + pressure) * motion[axis])
                for v in range(5):
                    if axis == 0:
                        ftmp[0, v, rows] = flux[v]
                    elif axis == 2:
                        ftmp[1, v, rows] = flux[v]
                    else:
                        total = weights[0] * flux[v]
                        for shift in range(1, 4):
                            total += weights[shift] * pltpu.roll(flux[v], 4 * shift, axis=0)
                        res[c, v, rows] = total
        for v in range(5):
            terms = [ftmp[0, v, 16 * i : 16 * i + 16] for i in range(4)]
            for a in range(4):
                total = res[c, v, 16 * a : 16 * a + 16]
                for i in range(4):
                    total += derivative[a][i] * terms[i]
                res[c, v, 16 * a : 16 * a + 16] = total
        for v in range(5):
            terms = [ftmp[1, v, pl.ds(k, 16, 4)] for k in range(4)]
            for a in range(4):
                total = res[c, v, pl.ds(a, 16, 4)]
                for k in range(4):
                    total += derivative[a][k] * terms[k]
                res[c, v, pl.ds(a, 16, 4)] = total
        return carry

    lax.fori_loop(0, TILES, volume_step, 0)

    def local_step(c, carry):
        span = pl.ds(pl.multiple_of(128 * c, 128), 128)
        for f in range(6):
            flux, speed = axis_flux(split(tr[f, c]), SIDE[f], 2.0 * (f % 2) - 1.0)
            for v in range(5):
                own[f, c, 16 * v : 16 * v + 16] = flux[v]
            spd[f, c] = speed
            tile, place = placed(partner_ref[f : f + 1, span])
            tile, place = wide(tile), wide(place)
            value = rest
            for t in range(TILES):
                value = jnp.where(
                    tile == (f ^ 1) * TILES + t, lanes_of(tr[f ^ 1, t], place), value
                )
            acc[f, c] = value
        return carry

    lax.fori_loop(0, TILES, local_step, 0)

    trace_copy(0).wait_recv()
    trace_copy(4).wait_recv()
    states = []
    for m in range(2):
        tile, place = placed(entry[m])
        tile, place = wide(tile), wide(place)
        value = mor[m]
        for p in (0, 4):
            value = jnp.where(tile == 24 + p, lanes_of(rcv[p], place), value)
        states.append(value)
    lane80 = wide(lane1)
    big = jnp.where(
        lane80 < 40,
        states[0],
        jnp.where(
            lane80 < 80,
            pltpu.roll(states[0], 40, axis=1),
            pltpu.roll(states[0], 80, axis=1),
        ),
    )
    near = jnp.dot(
        matrix_ref[0:320], big, precision=HIGHEST, preferred_element_type=jnp.float32
    )
    nears = [
        jnp.where(lane80 < 80, near[0:80], near[80:160]),
        jnp.where(lane80 < 40, near[160:240], near[240:320]),
    ]
    stars = []
    for m in range(2):
        normal = [
            wide(
                jnp.where(direction[m] == 2 * axis + 1, 1.0, 0.0)
                - jnp.where(direction[m] == 2 * axis, 1.0, 0.0),
                16,
            )
            for axis in range(3)
        ]
        inside, outside = split(nears[m]), split(states[m])
        inside_flux, inside_speed = normal_flux(inside, normal)
        outside_flux, outside_speed = normal_flux(outside, normal)
        half = 0.5 * jnp.maximum(inside_speed, outside_speed)
        stars.append(
            jnp.concatenate(
                [
                    0.5 * (inside_flux[v] + outside_flux[v]) - half * (outside[v] - inside[v])
                    for v in range(5)
                ],
                axis=0,
            )
        )
    home_a = jnp.dot(
        matrix_ref[320:480], stars[0], precision=HIGHEST, preferred_element_type=jnp.float32
    )
    home_b = jnp.dot(
        matrix_ref[480:640], stars[1], precision=HIGHEST, preferred_element_type=jnp.float32
    )
    together = (
        pltpu.roll(home_a[0:80], 88, axis=1)
        + pltpu.roll(home_a[80:160], 48, axis=1)
        + home_b[0:80]
        + pltpu.roll(home_b[80:160], 88, axis=1)
    )
    tab[0] = jnp.where(lane80 < 40, together, -stars[0])
    tab[1] = -stars[1]

    def return_copy(side):
        step = 1 - 2 * side
        return pltpu.make_async_remote_copy(
            src_ref=rsnd.at[side],
            dst_ref=rrcv.at[side],
            send_sem=rsend_sem.at[side],
            recv_sem=rrecv_sem.at[side],
            device_id=(lax.rem(me + step + count, count),),
            device_id_type=MESH,
        )

    quarter = jnp.right_shift(lane, 5)
    for side in range(2):
        index = wide(leaving[side : side + 1], 8)
        first = index < 120
        named = index < 200
        place = jnp.bitwise_and(jnp.where(first, index, index - 120), 127)
        for k in range(3):
            value = jnp.zeros((8, 128), jnp.float32)
            for b in range(4):
                g = 4 * k + b
                if g < 10:
                    rows = slice(8 * g, 8 * g + 8)
                    found = jnp.where(
                        first, lanes_of(tab[0, rows], place), lanes_of(tab[1, rows], place)
                    )
                    value = jnp.where((quarter == b) & named, found, value)
            rsnd[side, 8 * k : 8 * k + 8] = value
        return_copy(side).start()

    def arrive_step(k, carry):
        p = order(k)

        @pl.when(k >= 2)
        def _():
            trace_copy(p).wait_recv()

        def tile_step(c, inner):
            span = pl.ds(pl.multiple_of(128 * c, 128), 128)
            table = rcv[p]
            for f in range(6):
                tile, place = placed(partner_ref[f : f + 1, span])
                acc[f, c] = jnp.where(
                    wide(tile) == 24 + p, lanes_of(table, wide(place)), acc[f, c]
                )
            return inner

        lax.fori_loop(0, TILES, tile_step, 0)
        return carry

    lax.fori_loop(0, 8, arrive_step, 0)
    return_copy(0).wait_recv()
    return_copy(1).wait_recv()

    def final_step(c, carry):
        span = pl.ds(pl.multiple_of(128 * c, 128), 128)
        for f in range(6):
            here, there = tr[f, c], acc[f, c]
            inside, outside = split(here), split(there)
            flux, speed = axis_flux(outside, SIDE[f], 2.0 * (f % 2) - 1.0)
            half = 0.5 * jnp.maximum(spd[f, c], speed)
            jumps = [
                0.5 * (flux[v] - own[f, c, 16 * v : 16 * v + 16]) - half * (outside[v] - inside[v])
                for v in range(5)
            ]
            if f < 4:
                index = wide(source_ref[f : f + 1, span], 8)
                first, second_tile = index < 120, index < 200
                third = index < 233
                place = jnp.bitwise_and(jnp.where(first, index, index - 120), 127)
                back = jnp.bitwise_and(jnp.where(third, index - 201, index - 233), 31)
                backs = [back + 32 * b for b in range(4)]
                for v in range(5):
                    pieces = []
                    for g in (2 * v, 2 * v + 1):
                        rows = slice(8 * g, 8 * g + 8)
                        packs = slice(8 * (g // 4), 8 * (g // 4) + 8)
                        far = backs[g % 4]
                        mortar = jnp.where(
                            first,
                            lanes_of(tab[0, rows], place),
                            jnp.where(
                                second_tile,
                                lanes_of(tab[1, rows], place),
                                jnp.where(
                                    third,
                                    lanes_of(rrcv[0, packs], far),
                                    lanes_of(rrcv[1, packs], far),
                                ),
                            ),
                        )
                        half_rows = slice(8 * (g % 2), 8 * (g % 2) + 8)
                        pieces.append(
                            jnp.where(
                                index == 200, jumps[v][half_rows], mortar - own[f, c, rows]
                            )
                        )
                    jumps[v] = jnp.concatenate(pieces, axis=0)
            for v in range(5):
                lift = 6.0 * jumps[v]
                if f < 2:
                    res[c, v, 48 * f : 48 * f + 16] += lift
                elif f < 4:
                    jmp[v] = lift
                    for i in range(4):
                        at = 16 * i + 12 * (f - 2)
                        res[c, v, at : at + 4] += jmp[v, 4 * i : 4 * i + 4]
                else:
                    res[c, v, pl.ds(3 * (f - 4), 16, 4)] += lift
        scale = -jnp.exp2(levels_ref[0:1, span].astype(jnp.float32) + 1.0)
        for v in range(5):
            out_ref[v, :, span] = wide(scale, 64) * res[c, v]
        return carry

    lax.fori_loop(0, TILES, final_step, 0)

    for p in range(8):
        trace_copy(p).wait_send()
    for side in range(2):
        return_copy(side).wait_send()


def body(
    state, step_size, levels, send_faces, partner, mortar_in, mortar_dir, return_faces, flux_source
):


    count = lax.axis_size("dev")
    vmem = pl.BlockSpec(memory_space=pltpu.VMEM)
    f32 = jnp.float32
    residual = pl.pallas_call(
        functools.partial(kernel, count),
        out_shape=jax.ShapeDtypeStruct(state.shape, f32),
        in_specs=[pl.BlockSpec(memory_space=pl.ANY)] + [vmem] * 8,
        out_specs=vmem,
        scratch_shapes=[
            pltpu.VMEM((TILES, 5, 64, 128), f32),
            pltpu.VMEM((6, TILES, 80, 128), f32),
            pltpu.VMEM((8, 80, 128), f32),
            pltpu.VMEM((8, 80, 128), f32),
            pltpu.VMEM((6, TILES, 80, 128), f32),
            pltpu.VMEM((6, TILES, 80, 128), f32),
            pltpu.VMEM((6, TILES, 16, 128), f32),
            pltpu.VMEM((TILES, 5, 64, 128), f32),
            pltpu.VMEM((2, 5, 64, 128), f32),
            pltpu.VMEM((2, 80, 128), f32),
            pltpu.VMEM((2, 80, 128), f32),
            pltpu.VMEM((2, 24, 128), f32),
            pltpu.VMEM((2, 24, 128), f32),
            pltpu.VMEM((8, 128), jnp.int32),
            pltpu.VMEM((5, 16, 128), f32),
            pltpu.SemaphoreType.DMA((TILES,)),
            pltpu.SemaphoreType.DMA((8,)),
            pltpu.SemaphoreType.DMA((8,)),
            pltpu.SemaphoreType.DMA((2,)),
            pltpu.SemaphoreType.DMA((2,)),
        ],
        compiler_params=pltpu.CompilerParams(
            collective_id=0, has_side_effects=True, vmem_limit_bytes=24 * 1024 * 1024
        ),
        name="section",
    )(
        state,
        levels.reshape(1, -1),
        send_faces,
        partner,
        mortar_in,
        mortar_dir.reshape(1, -1),
        return_faces,
        flux_source,
        jnp.asarray(mortar_matrices()),
    )
    return step_size[0] * residual


def solution(mesh):
    placed = (
        P(None, None, "dev"),
        P(),
        P("dev"),
        P("dev", None),
        P(None, "dev"),
        P(None, "dev"),
        P("dev"),
        P("dev", None),
        P(None, "dev"),
    )
    return jax.shard_map(
        body, mesh=mesh, in_specs=placed, out_specs=P(None, None, "dev"), check_vma=False
    )
```

```python
import functools

import jax
import jax.numpy as jnp
import numpy as np
from jax import lax
from jax.experimental import pallas as pl
from jax.experimental.pallas import tpu as pltpu
from jax.sharding import PartitionSpec as P

GAMMA = 1.4
HIGHEST = lax.Precision.HIGHEST
MESH = pl.DeviceIdType.MESH
TILES = 4
SIDE = (0, 0, 1, 1, 2, 2)


def lobatto_tables():
    nodes = np.array([-1.0, -1.0 / np.sqrt(5.0), 1.0 / np.sqrt(5.0), 1.0])
    weights = np.array([1.0, 5.0, 5.0, 1.0]) / 6.0

    def basis(points):
        table = np.ones((len(points), 4))
        for column in range(4):
            for other in range(4):
                if other != column:
                    table[:, column] *= (points - nodes[other]) / (nodes[column] - nodes[other])
        return table

    derivative = np.zeros((4, 4))
    for row in range(4):
        for column in range(4):
            total = 0.0
            for other in range(4):
                if other != column:
                    term = 1.0 / (nodes[column] - nodes[other])
                    for third in range(4):
                        if third != column and third != other:
                            term *= (nodes[row] - nodes[third]) / (nodes[column] - nodes[third])
                    total += term
            derivative[row, column] = total
    lower = basis((nodes - 1.0) / 2.0)
    upper = basis((nodes + 1.0) / 2.0)
    back_lower = 0.5 * (lower.T * weights[None, :]) / weights[:, None]
    back_upper = 0.5 * (upper.T * weights[None, :]) / weights[:, None]
    return [
        np.asarray(table, np.float32)
        for table in (derivative, lower, upper, back_lower, back_upper)
    ]


def mortar_matrices():
    _, lower, upper, back_lower, back_upper = [t.astype(np.float64) for t in lobatto_tables()]
    ahead, back = (lower, upper), (back_lower, back_upper)
    five = np.eye(5)
    forth = [np.kron(five, np.kron(ahead[q % 2], ahead[q // 2])) for q in range(4)]
    home = [np.kron(five, np.kron(back[q % 2], back[q // 2])) for q in range(4)]
    return np.concatenate(forth + home, axis=0).astype(np.float32)


def lanes_of(tile, index):
    return jnp.take_along_axis(tile, index, axis=1, mode="promise_in_bounds")


def axis_flux(parts, axis, sign):
    density, energy = parts[0], parts[4]
    inverse = 1.0 / density
    along = sign * parts[1 + axis] * inverse
    kinetic = parts[1] * parts[1] + parts[2] * parts[2] + parts[3] * parts[3]
    pressure = (GAMMA - 1.0) * (energy - 0.5 * kinetic * inverse)
    flux = [density * along]
    for other in range(3):
        term = parts[1 + other] * along
        flux.append(term + sign * pressure if other == axis else term)
    flux.append((energy + pressure) * along)
    speed = jnp.abs(along) + jnp.sqrt(GAMMA * pressure * inverse)
    return flux, speed


def normal_flux(parts, normal):
    density, energy = parts[0], parts[4]
    motion = [parts[1 + axis] / density for axis in range(3)]
    pressure = (GAMMA - 1.0) * (
        energy - 0.5 * (parts[1] * motion[0] + parts[2] * motion[1] + parts[3] * motion[2])
    )
    along = motion[0] * normal[0] + motion[1] * normal[1] + motion[2] * normal[2]
    flux = [density * along]
    for axis in range(3):
        flux.append(parts[1 + axis] * along + pressure * normal[axis])
    flux.append((energy + pressure) * along)
    speed = jnp.abs(along) + jnp.sqrt(GAMMA * pressure / density)
    return flux, speed


def split(columns):
    return [columns[16 * v : 16 * v + 16] for v in range(5)]


def rest_state():
    row = lax.broadcasted_iota(jnp.int32, (80, 128), 0)
    return jnp.where(row < 16, 1.0, jnp.where(row >= 64, 2.5, 0.0)).astype(jnp.float32)


def kernel(
    count,
    state_hbm,
    levels_hbm,
    send_hbm,
    partner_hbm,
    mortar_hbm,
    dir_hbm,
    return_hbm,
    source_hbm,
    matrix_hbm,
    out_ref,
    levels_ref,
    send_ref,
    partner_ref,
    mortar_ref,
    dir_ref,
    return_ref,
    source_ref,
    matrix_ref,
    st,
    tr,
    snd,
    rcv,
    acc,
    own,
    spd,
    res,
    ftmp,
    mor,
    tab,
    rsnd,
    rrcv,
    pad,
    lift_j,
    lift_k,
    load_sem,
    small_sem,
    send_sem,
    recv_sem,
    rsend_sem,
    rrecv_sem,
):
    me = lax.axis_index("dev")
    derivative = [[float(x) for x in row] for row in lobatto_tables()[0]]

    def peer_of(p):
        offset = jnp.where(p < 4, p + 1, 3 - p)
        return lax.rem(me + offset + count, count)

    barrier = pltpu.get_barrier_semaphore()
    for p in range(8):
        pl.semaphore_signal(barrier, inc=1, device_id=(peer_of(p),), device_id_type=MESH)

    def load_of(c):
        span = pl.ds(pl.multiple_of(128 * c, 128), 128)
        return pltpu.make_async_copy(state_hbm.at[:, :, span], st.at[c], load_sem.at[c])

    for c in range(TILES):
        load_of(c).start()
    small = [
        pltpu.make_async_copy(source, target, small_sem.at[n])
        for n, (source, target) in enumerate(
            (
                (send_hbm, send_ref),
                (mortar_hbm, mortar_ref),
                (dir_hbm, dir_ref),
                (return_hbm, return_ref),
                (partner_hbm, partner_ref),
                (source_hbm, source_ref),
                (levels_hbm, levels_ref),
                (matrix_hbm, matrix_ref),
            )
        )
    ]
    for load in small:
        load.start()

    lane = lax.broadcasted_iota(jnp.int32, (8, 128), 1)
    lane1 = lane[0:1]
    rest = rest_state()

    def placed(index):
        moved = jnp.where(index > 3072, index - 1, index)
        tile = jnp.where(index == 3072, -1, jnp.right_shift(moved, 7))
        return tile, jnp.bitwise_and(moved, 127)

    def wide(row, rows=80):
        return jnp.broadcast_to(row, (rows, 128))

    def trace_step(c, carry):
        load_of(c).wait()
        for v in range(5):
            tr[0, c, 16 * v : 16 * v + 16] = st[c, v, 0:16]
            tr[1, c, 16 * v : 16 * v + 16] = st[c, v, 48:64]
            for i in range(4):
                tr[2, c, 16 * v + 4 * i : 16 * v + 4 * i + 4] = st[c, v, 16 * i : 16 * i + 4]
                tr[3, c, 16 * v + 4 * i : 16 * v + 4 * i + 4] = st[c, v, 16 * i + 12 : 16 * i + 16]
            tr[4, c, 16 * v : 16 * v + 16] = st[c, v, pl.ds(0, 16, 4)]
            tr[5, c, 16 * v : 16 * v + 16] = st[c, v, pl.ds(3, 16, 4)]
        return carry

    lax.fori_loop(0, TILES, trace_step, 0)


    def trace_copy(p):
        return pltpu.make_async_remote_copy(
            src_ref=snd.at[p],
            dst_ref=rcv.at[p],
            send_sem=send_sem.at[p],
            recv_sem=recv_sem.at[p],
            device_id=(peer_of(p),),
            device_id_type=MESH,
        )

    def order(k):
        return lax.rem(k, 2) * 4 + lax.rem(4 - k // 2, 4)

    row16 = lax.broadcasted_iota(jnp.int32, (16, 128), 0)
    second = jnp.right_shift(row16, 2)

    def by_row(shift):
        picks = [derivative[j][(j - shift) % 4] for j in range(4)]
        return jnp.where(
            second == 0,
            picks[0],
            jnp.where(second == 1, picks[1], jnp.where(second == 2, picks[2], picks[3])),
        ).astype(jnp.float32)

    weights = [by_row(shift) for shift in range(4)]

    def fluxes_of(c):
        for i in range(4):
            rows = pl.ds(16 * i, 16)
            parts = [st[c, v, rows] for v in range(5)]
            inverse = 1.0 / parts[0]
            motion = [parts[1 + a] * inverse for a in range(3)]
            pressure = (GAMMA - 1.0) * (
                parts[4]
                - 0.5 * (parts[1] * motion[0] + parts[2] * motion[1] + parts[3] * motion[2])
            )
            for axis in range(3):
                flux = [parts[1 + axis]]
                for other in range(3):
                    term = parts[1 + other] * motion[axis]
                    flux.append(term + pressure if other == axis else term)
                flux.append((parts[4] + pressure) * motion[axis])
                for v in range(5):
                    if axis == 0:
                        ftmp[0, v, rows] = flux[v]
                    elif axis == 2:
                        ftmp[1, v, rows] = flux[v]
                    else:
                        total = weights[0] * flux[v]
                        for shift in range(1, 4):
                            total += weights[shift] * pltpu.roll(flux[v], 4 * shift, axis=0)
                        res[c, v, rows] = total

    def slopes_of(c):
        for v in range(5):
            terms = [ftmp[0, v, 16 * i : 16 * i + 16] for i in range(4)]
            for a in range(4):
                total = res[c, v, 16 * a : 16 * a + 16]
                for i in range(4):
                    total += derivative[a][i] * terms[i]
                res[c, v, 16 * a : 16 * a + 16] = total
        for v in range(5):
            terms = [ftmp[1, v, pl.ds(k, 16, 4)] for k in range(4)]
            for a in range(4):
                total = res[c, v, pl.ds(a, 16, 4)]
                for k in range(4):
                    total += derivative[a][k] * terms[k]
                res[c, v, pl.ds(a, 16, 4)] = total

    def own_fluxes_of(c):
        for f in range(6):
            flux, speed = axis_flux(split(tr[f, c]), SIDE[f], 2.0 * (f % 2) - 1.0)
            for v in range(5):
                own[f, c, 16 * v : 16 * v + 16] = flux[v]
            spd[f, c] = speed

    def outgoing(p):
        index = send_ref[pl.ds(p, 1), :]
        tile = wide(jnp.right_shift(index, 7))
        place = wide(jnp.bitwise_and(index, 127))
        value = rest
        for f in range(6):
            for c in range(TILES):
                value = jnp.where(tile == f * TILES + c, lanes_of(tr[f, c], place), value)
        snd[p] = value

    def send_step(c, carry):
        p = lax.rem(4 - c, 4)
        outgoing(p)
        fluxes_of(c)
        outgoing(p + 4)
        slopes_of(c)
        own_fluxes_of(c)
        for v in range(5):
            lift_j[c, v] = jnp.zeros((64, 128), jnp.float32)
            lift_k[c, v] = jnp.zeros((64, 128), jnp.float32)
        return carry

    small[0].wait()
    lax.fori_loop(0, TILES, send_step, 0)
    pl.semaphore_wait(barrier, 8)
    for p in (0, 4):
        trace_copy(p).start()

    for n in (1, 2, 3):
        small[n].wait()
    pad[...] = jnp.full((8, 128), 3072, jnp.int32)
    pad[0:5, 0:40] = mortar_ref[...]
    pad[5:6, 0:40] = dir_ref[...]
    pad[6:8, 0:32] = return_ref[...]
    packed = pad[...]
    by40 = pltpu.roll(packed, 40, axis=1)
    by80 = pltpu.roll(packed, 80, axis=1)
    entry = [
        jnp.where(
            lane1 < 40,
            packed[0:1],
            jnp.where(lane1 < 80, by40[1:2], jnp.where(lane1 < 120, by80[2:3], 3072)),
        ),
        jnp.where(lane1 < 40, packed[3:4], jnp.where(lane1 < 80, by40[4:5], 3072)),
    ]
    direction = [
        jnp.where(lane1 < 40, packed[5:6], jnp.where(lane1 < 80, by40[5:6], by80[5:6])),
        jnp.where(lane1 < 40, packed[5:6], by40[5:6]),
    ]
    by32 = pltpu.roll(packed, 32, axis=1)
    by64 = pltpu.roll(packed, 64, axis=1)
    by96 = pltpu.roll(packed, 96, axis=1)
    leaving = jnp.where(
        lane < 32, packed, jnp.where(lane < 64, by32, jnp.where(lane < 96, by64, by96))
    )[6:8]

    for m in range(2):
        tile, place = placed(entry[m])
        tile, place = wide(tile), wide(place)
        value = rest
        for f in range(4):
            for c in range(TILES):
                value = jnp.where(tile == f * TILES + c, lanes_of(tr[f, c], place), value)
        mor[m] = value

    for p in (3, 7, 2, 6, 1, 5):
        trace_copy(p).start()
    trace_copy(0).wait_recv()
    trace_copy(4).wait_recv()
    small[7].wait()
    states = []
    for m in range(2):
        tile, place = placed(entry[m])
        tile, place = wide(tile), wide(place)
        value = mor[m]
        for p in (0, 4):
            value = jnp.where(tile == 24 + p, lanes_of(rcv[p], place), value)
        states.append(value)
    lane80 = wide(lane1)
    big = jnp.where(
        lane80 < 40,
        states[0],
        jnp.where(
            lane80 < 80,
            pltpu.roll(states[0], 40, axis=1),
            pltpu.roll(states[0], 80, axis=1),
        ),
    )
    near = jnp.dot(
        matrix_ref[0:320], big, precision=HIGHEST, preferred_element_type=jnp.float32
    )
    nears = [
        jnp.where(lane80 < 80, near[0:80], near[80:160]),
        jnp.where(lane80 < 40, near[160:240], near[240:320]),
    ]
    stars = []
    for m in range(2):
        normal = [
            wide(
                jnp.where(direction[m] == 2 * axis + 1, 1.0, 0.0)
                - jnp.where(direction[m] == 2 * axis, 1.0, 0.0),
                16,
            )
            for axis in range(3)
        ]
        inside, outside = split(nears[m]), split(states[m])
        inside_flux, inside_speed = normal_flux(inside, normal)
        outside_flux, outside_speed = normal_flux(outside, normal)
        half = 0.5 * jnp.maximum(inside_speed, outside_speed)
        stars.append(
            jnp.concatenate(
                [
                    0.5 * (inside_flux[v] + outside_flux[v]) - half * (outside[v] - inside[v])
                    for v in range(5)
                ],
                axis=0,
            )
        )
    home_a = jnp.dot(
        matrix_ref[320:480], stars[0], precision=HIGHEST, preferred_element_type=jnp.float32
    )
    home_b = jnp.dot(
        matrix_ref[480:640], stars[1], precision=HIGHEST, preferred_element_type=jnp.float32
    )
    together = (
        pltpu.roll(home_a[0:80], 88, axis=1)
        + pltpu.roll(home_a[80:160], 48, axis=1)
        + home_b[0:80]
        + pltpu.roll(home_b[80:160], 88, axis=1)
    )
    tab[0] = jnp.where(lane80 < 40, together, -stars[0])
    tab[1] = -stars[1]

    def return_copy(side):
        step = 1 - 2 * side
        return pltpu.make_async_remote_copy(
            src_ref=rsnd.at[side],
            dst_ref=rrcv.at[side],
            send_sem=rsend_sem.at[side],
            recv_sem=rrecv_sem.at[side],
            device_id=(lax.rem(me + step + count, count),),
            device_id_type=MESH,
        )

    quarter = jnp.right_shift(lane, 5)
    for side in range(2):
        index = wide(leaving[side : side + 1], 8)
        first = index < 120
        named = index < 200
        place = jnp.bitwise_and(jnp.where(first, index, index - 120), 127)
        for k in range(3):
            value = jnp.zeros((8, 128), jnp.float32)
            for b in range(4):
                g = 4 * k + b
                if g < 10:
                    rows = slice(8 * g, 8 * g + 8)
                    found = jnp.where(
                        first, lanes_of(tab[0, rows], place), lanes_of(tab[1, rows], place)
                    )
                    value = jnp.where((quarter == b) & named, found, value)
            rsnd[side, 8 * k : 8 * k + 8] = value
        return_copy(side).start()

    small[4].wait()

    def local_step(c, carry):
        span = pl.ds(pl.multiple_of(128 * c, 128), 128)
        for f in range(6):
            tile, place = placed(partner_ref[f : f + 1, span])
            tile, place = wide(tile), wide(place)
            value = rest
            for t in range(TILES):
                value = jnp.where(
                    tile == (f ^ 1) * TILES + t, lanes_of(tr[f ^ 1, t], place), value
                )
            acc[f, c] = value
        return carry

    lax.fori_loop(0, TILES, local_step, 0)

    def arrive_step(k, carry):
        p = lax.rem(4 - k, 4)

        @pl.when(k >= 1)
        def _():
            trace_copy(p).wait_recv()
            trace_copy(p + 4).wait_recv()

        for c in range(TILES):
            for f in range(6):
                tile, place = placed(partner_ref[f : f + 1, 128 * c : 128 * c + 128])
                tile, place = wide(tile), wide(place)
                value = acc[f, c]
                for q in (p, p + 4):
                    value = jnp.where(tile == 24 + q, lanes_of(rcv[q], place), value)
                acc[f, c] = value
        return carry

    lax.fori_loop(0, 4, arrive_step, 0)
    return_copy(0).wait_recv()
    return_copy(1).wait_recv()
    small[5].wait()
    small[6].wait()

    for c in range(TILES):
        span = slice(128 * c, 128 * c + 128)
        ends = [[None] * 5, [None] * 5]
        for f in range(6):
            here, there = tr[f, c], acc[f, c]
            inside, outside = split(here), split(there)
            flux, speed = axis_flux(outside, SIDE[f], 2.0 * (f % 2) - 1.0)
            half = 0.5 * jnp.maximum(spd[f, c], speed)
            jumps = [
                0.5 * (flux[v] - own[f, c, 16 * v : 16 * v + 16]) - half * (outside[v] - inside[v])
                for v in range(5)
            ]
            if f < 4:
                index = wide(source_ref[f : f + 1, span], 8)
                first, second_tile = index < 120, index < 200
                third = index < 233
                place = jnp.bitwise_and(jnp.where(first, index, index - 120), 127)
                back = jnp.bitwise_and(jnp.where(third, index - 201, index - 233), 31)
                backs = [back + 32 * b for b in range(4)]
                for v in range(5):
                    pieces = []
                    for g in (2 * v, 2 * v + 1):
                        rows = slice(8 * g, 8 * g + 8)
                        packs = slice(8 * (g // 4), 8 * (g // 4) + 8)
                        far = backs[g % 4]
                        mortar = jnp.where(
                            first,
                            lanes_of(tab[0, rows], place),
                            jnp.where(
                                second_tile,
                                lanes_of(tab[1, rows], place),
                                jnp.where(
                                    third,
                                    lanes_of(rrcv[0, packs], far),
                                    lanes_of(rrcv[1, packs], far),
                                ),
                            ),
                        )
                        half_rows = slice(8 * (g % 2), 8 * (g % 2) + 8)
                        pieces.append(
                            jnp.where(
                                index == 200, jumps[v][half_rows], mortar - own[f, c, rows]
                            )
                        )
                    jumps[v] = jnp.concatenate(pieces, axis=0)
            for v in range(5):
                if f < 2:
                    ends[f][v] = jumps[v]
                elif f < 4:
                    for i in range(4):
                        at = 16 * i + 12 * (f - 2)
                        lift_j[c, v, at : at + 4] = jumps[v][4 * i : 4 * i + 4]
                else:
                    lift_k[c, v, pl.ds(3 * (f - 4), 16, 4)] = jumps[v]
        scale = -jnp.exp2(levels_ref[0:1, span].astype(jnp.float32) + 1.0)
        for v in range(5):
            for i in range(4):
                rows = slice(16 * i, 16 * i + 16)
                lift = lift_j[c, v, rows] + lift_k[c, v, rows]
                if i in (0, 3):
                    lift += ends[i // 3][v]
                out_ref[v, rows, span] = wide(scale, 16) * (res[c, v, rows] + 6.0 * lift)

    for p in range(8):
        trace_copy(p).wait_send()
    for side in range(2):
        return_copy(side).wait_send()


def body(
    state, step_size, levels, send_faces, partner, mortar_in, mortar_dir, return_faces, flux_source
):


    count = lax.axis_size("dev")
    vmem = pl.BlockSpec(memory_space=pltpu.VMEM)
    f32 = jnp.float32
    residual = pl.pallas_call(
        functools.partial(kernel, count),
        out_shape=jax.ShapeDtypeStruct(state.shape, f32),
        in_specs=[pl.BlockSpec(memory_space=pltpu.HBM)] * 9,
        out_specs=vmem,
        scratch_shapes=[
            pltpu.VMEM((1, 512), jnp.int32),
            pltpu.VMEM((8, 128), jnp.int32),
            pltpu.VMEM((6, 512), jnp.int32),
            pltpu.VMEM((5, 40), jnp.int32),
            pltpu.VMEM((1, 40), jnp.int32),
            pltpu.VMEM((2, 32), jnp.int32),
            pltpu.VMEM((6, 512), jnp.int32),
            pltpu.VMEM((640, 80), f32),
            pltpu.VMEM((TILES, 5, 64, 128), f32),
            pltpu.VMEM((6, TILES, 80, 128), f32),
            pltpu.VMEM((8, 80, 128), f32),
            pltpu.VMEM((8, 80, 128), f32),
            pltpu.VMEM((6, TILES, 80, 128), f32),
            pltpu.VMEM((6, TILES, 80, 128), f32),
            pltpu.VMEM((6, TILES, 16, 128), f32),
            pltpu.VMEM((TILES, 5, 64, 128), f32),
            pltpu.VMEM((2, 5, 64, 128), f32),
            pltpu.VMEM((2, 80, 128), f32),
            pltpu.VMEM((2, 80, 128), f32),
            pltpu.VMEM((2, 24, 128), f32),
            pltpu.VMEM((2, 24, 128), f32),
            pltpu.VMEM((8, 128), jnp.int32),
            pltpu.VMEM((TILES, 5, 64, 128), f32),
            pltpu.VMEM((TILES, 5, 64, 128), f32),
            pltpu.SemaphoreType.DMA((TILES,)),
            pltpu.SemaphoreType.DMA((8,)),
            pltpu.SemaphoreType.DMA((8,)),
            pltpu.SemaphoreType.DMA((8,)),
            pltpu.SemaphoreType.DMA((2,)),
            pltpu.SemaphoreType.DMA((2,)),
        ],
        compiler_params=pltpu.CompilerParams(
            collective_id=0, has_side_effects=True, vmem_limit_bytes=24 * 1024 * 1024
        ),
        name="section",
    )(
        *(
            pltpu.with_memory_space_constraint(array, pltpu.HBM)
            for array in (
                state,
                levels.reshape(1, -1),
                send_faces,
                partner,
                mortar_in,
                mortar_dir.reshape(1, -1),
                return_faces,
                flux_source,
                jnp.asarray(mortar_matrices()),
            )
        )
    )
    return step_size[0] * residual


def solution(mesh):
    placed = (
        P(None, None, "dev"),
        P(),
        P("dev"),
        P("dev", None),
        P(None, "dev"),
        P(None, "dev"),
        P("dev"),
        P("dev", None),
        P(None, "dev"),
    )
    return jax.shard_map(
        body, mesh=mesh, in_specs=placed, out_specs=P(None, None, "dev"), check_vma=False
    )
```

```python
import functools

import jax
import jax.numpy as jnp
import numpy as np
from jax import lax
from jax.experimental import pallas as pl
from jax.experimental.pallas import tpu as pltpu
from jax.sharding import PartitionSpec as P

GAMMA = 1.4
HIGHEST = lax.Precision.HIGHEST
MESH = pl.DeviceIdType.MESH
TILES = 4
SIDE = (0, 0, 1, 1, 2, 2)


def lobatto_tables():
    nodes = np.array([-1.0, -1.0 / np.sqrt(5.0), 1.0 / np.sqrt(5.0), 1.0])
    weights = np.array([1.0, 5.0, 5.0, 1.0]) / 6.0

    def basis(points):
        table = np.ones((len(points), 4))
        for column in range(4):
            for other in range(4):
                if other != column:
                    table[:, column] *= (points - nodes[other]) / (nodes[column] - nodes[other])
        return table

    derivative = np.zeros((4, 4))
    for row in range(4):
        for column in range(4):
            total = 0.0
            for other in range(4):
                if other != column:
                    term = 1.0 / (nodes[column] - nodes[other])
                    for third in range(4):
                        if third != column and third != other:
                            term *= (nodes[row] - nodes[third]) / (nodes[column] - nodes[third])
                    total += term
            derivative[row, column] = total
    lower = basis((nodes - 1.0) / 2.0)
    upper = basis((nodes + 1.0) / 2.0)
    back_lower = 0.5 * (lower.T * weights[None, :]) / weights[:, None]
    back_upper = 0.5 * (upper.T * weights[None, :]) / weights[:, None]
    return [
        np.asarray(table, np.float32)
        for table in (derivative, lower, upper, back_lower, back_upper)
    ]


def mortar_matrices():
    _, lower, upper, back_lower, back_upper = [t.astype(np.float64) for t in lobatto_tables()]
    ahead, back = (lower, upper), (back_lower, back_upper)
    five = np.eye(5)
    forth = [np.kron(five, np.kron(ahead[q % 2], ahead[q // 2])) for q in range(4)]
    home = [np.kron(five, np.kron(back[q % 2], back[q // 2])) for q in range(4)]
    return np.concatenate(forth + home, axis=0).astype(np.float32)


def lanes_of(tile, index):
    return jnp.take_along_axis(tile, index, axis=1, mode="promise_in_bounds")


def axis_flux(parts, axis, sign):
    density, energy = parts[0], parts[4]
    inverse = 1.0 / density
    along = sign * parts[1 + axis] * inverse
    kinetic = parts[1] * parts[1] + parts[2] * parts[2] + parts[3] * parts[3]
    pressure = (GAMMA - 1.0) * (energy - 0.5 * kinetic * inverse)
    flux = [density * along]
    for other in range(3):
        term = parts[1 + other] * along
        flux.append(term + sign * pressure if other == axis else term)
    flux.append((energy + pressure) * along)
    speed = jnp.abs(along) + jnp.sqrt(GAMMA * pressure * inverse)
    return flux, speed


def normal_flux(parts, normal):
    density, energy = parts[0], parts[4]
    motion = [parts[1 + axis] / density for axis in range(3)]
    pressure = (GAMMA - 1.0) * (
        energy - 0.5 * (parts[1] * motion[0] + parts[2] * motion[1] + parts[3] * motion[2])
    )
    along = motion[0] * normal[0] + motion[1] * normal[1] + motion[2] * normal[2]
    flux = [density * along]
    for axis in range(3):
        flux.append(parts[1 + axis] * along + pressure * normal[axis])
    flux.append((energy + pressure) * along)
    speed = jnp.abs(along) + jnp.sqrt(GAMMA * pressure / density)
    return flux, speed


def split(columns):
    return [columns[16 * v : 16 * v + 16] for v in range(5)]


def rest_state():
    row = lax.broadcasted_iota(jnp.int32, (80, 128), 0)
    return jnp.where(row < 16, 1.0, jnp.where(row >= 64, 2.5, 0.0)).astype(jnp.float32)


def kernel(
    count,
    state_hbm,
    levels_hbm,
    send_hbm,
    partner_hbm,
    mortar_hbm,
    dir_hbm,
    return_hbm,
    source_hbm,
    matrix_hbm,
    res,
    own,
    rrcv,
    source_ref,
    levels_ref,
    send_ref,
    partner_ref,
    mortar_ref,
    dir_ref,
    return_ref,
    matrix_ref,
    st,
    tr,
    snd,
    rcv,
    acc,
    spd,
    ftmp,
    mor,
    tab,
    rsnd,
    pad,
    hang,
    lift_j,
    lift_k,
    load_sem,
    small_sem,
    send_sem,
    recv_sem,
    rsend_sem,
    rrecv_sem,
):
    me = lax.axis_index("dev")
    derivative = [[float(x) for x in row] for row in lobatto_tables()[0]]

    def peer_of(p):
        offset = jnp.where(p < 4, p + 1, 3 - p)
        return lax.rem(me + offset + count, count)

    barrier = pltpu.get_barrier_semaphore()
    for p in range(8):
        pl.semaphore_signal(barrier, inc=1, device_id=(peer_of(p),), device_id_type=MESH)

    def load_of(c):
        span = pl.ds(pl.multiple_of(128 * c, 128), 128)
        return pltpu.make_async_copy(state_hbm.at[:, :, span], st.at[c], load_sem.at[c])

    for c in range(TILES):
        load_of(c).start()
    small = [
        pltpu.make_async_copy(source, target, small_sem.at[n])
        for n, (source, target) in enumerate(
            (
                (send_hbm, send_ref),
                (mortar_hbm, mortar_ref),
                (dir_hbm, dir_ref),
                (return_hbm, return_ref),
                (partner_hbm, partner_ref),
                (source_hbm, source_ref),
                (levels_hbm, levels_ref),
                (matrix_hbm, matrix_ref),
            )
        )
    ]
    for load in small:
        load.start()

    lane = lax.broadcasted_iota(jnp.int32, (8, 128), 1)
    lane1 = lane[0:1]
    rest = rest_state()

    def placed(index):
        moved = jnp.where(index > 3072, index - 1, index)
        tile = jnp.where(index == 3072, -1, jnp.right_shift(moved, 7))
        return tile, jnp.bitwise_and(moved, 127)

    def wide(row, rows=80):
        return jnp.broadcast_to(row, (rows, 128))

    def trace_step(c, carry):
        load_of(c).wait()
        for v in range(5):
            tr[0, c, 16 * v : 16 * v + 16] = st[c, v, 0:16]
            tr[1, c, 16 * v : 16 * v + 16] = st[c, v, 48:64]
            for i in range(4):
                tr[2, c, 16 * v + 4 * i : 16 * v + 4 * i + 4] = st[c, v, 16 * i : 16 * i + 4]
                tr[3, c, 16 * v + 4 * i : 16 * v + 4 * i + 4] = st[c, v, 16 * i + 12 : 16 * i + 16]
            tr[4, c, 16 * v : 16 * v + 16] = st[c, v, pl.ds(0, 16, 4)]
            tr[5, c, 16 * v : 16 * v + 16] = st[c, v, pl.ds(3, 16, 4)]
        return carry

    lax.fori_loop(0, TILES, trace_step, 0)


    def trace_copy(p):
        return pltpu.make_async_remote_copy(
            src_ref=snd.at[p],
            dst_ref=rcv.at[p],
            send_sem=send_sem.at[p],
            recv_sem=recv_sem.at[p],
            device_id=(peer_of(p),),
            device_id_type=MESH,
        )

    def order(k):
        return lax.rem(k, 2) * 4 + lax.rem(4 - k // 2, 4)

    row16 = lax.broadcasted_iota(jnp.int32, (16, 128), 0)
    second = jnp.right_shift(row16, 2)

    def by_row(shift):
        picks = [derivative[j][(j - shift) % 4] for j in range(4)]
        return jnp.where(
            second == 0,
            picks[0],
            jnp.where(second == 1, picks[1], jnp.where(second == 2, picks[2], picks[3])),
        ).astype(jnp.float32)

    weights = [by_row(shift) for shift in range(4)]

    def fluxes_of(c):
        for i in range(4):
            rows = pl.ds(16 * i, 16)
            parts = [st[c, v, rows] for v in range(5)]
            inverse = 1.0 / parts[0]
            motion = [parts[1 + a] * inverse for a in range(3)]
            pressure = (GAMMA - 1.0) * (
                parts[4]
                - 0.5 * (parts[1] * motion[0] + parts[2] * motion[1] + parts[3] * motion[2])
            )
            for axis in range(3):
                flux = [parts[1 + axis]]
                for other in range(3):
                    term = parts[1 + other] * motion[axis]
                    flux.append(term + pressure if other == axis else term)
                flux.append((parts[4] + pressure) * motion[axis])
                for v in range(5):
                    if axis == 0:
                        ftmp[0, v, rows] = flux[v]
                    elif axis == 2:
                        ftmp[1, v, rows] = flux[v]
                    else:
                        total = weights[0] * flux[v]
                        for shift in range(1, 4):
                            total += weights[shift] * pltpu.roll(flux[v], 4 * shift, axis=0)
                        res[c, v, rows] = total

    def slopes_of(c):
        for v in range(5):
            terms = [ftmp[0, v, 16 * i : 16 * i + 16] for i in range(4)]
            for a in range(4):
                total = res[c, v, 16 * a : 16 * a + 16]
                for i in range(4):
                    total += derivative[a][i] * terms[i]
                res[c, v, 16 * a : 16 * a + 16] = total
        for v in range(5):
            terms = [ftmp[1, v, pl.ds(k, 16, 4)] for k in range(4)]
            for a in range(4):
                total = res[c, v, pl.ds(a, 16, 4)]
                for k in range(4):
                    total += derivative[a][k] * terms[k]
                res[c, v, pl.ds(a, 16, 4)] = total

    def own_fluxes_of(c):
        for f in range(6):
            flux, speed = axis_flux(split(tr[f, c]), SIDE[f], 2.0 * (f % 2) - 1.0)
            for v in range(5):
                own[f, c, 16 * v : 16 * v + 16] = flux[v]
            spd[f, c] = speed

    def outgoing(p):
        index = send_ref[pl.ds(p, 1), :]
        tile = wide(jnp.right_shift(index, 7))
        place = wide(jnp.bitwise_and(index, 127))
        value = rest
        for f in range(6):
            for c in range(TILES):
                value = jnp.where(tile == f * TILES + c, lanes_of(tr[f, c], place), value)
        snd[p] = value

    def send_step(c, carry):
        p = lax.rem(4 - c, 4)
        outgoing(p)
        fluxes_of(c)
        outgoing(p + 4)
        slopes_of(c)
        own_fluxes_of(c)
        for v in range(5):
            lift_j[c, v] = jnp.zeros((64, 128), jnp.float32)
            lift_k[c, v] = jnp.zeros((64, 128), jnp.float32)
        return carry

    small[0].wait()
    lax.fori_loop(0, TILES, send_step, 0)
    pl.semaphore_wait(barrier, 8)
    for p in (4, 0):
        trace_copy(p).start()

    for n in (1, 2, 3):
        small[n].wait()
    pad[...] = jnp.full((8, 128), 3072, jnp.int32)
    pad[0:5, 0:40] = mortar_ref[...]
    pad[5:6, 0:40] = dir_ref[...]
    pad[6:8, 0:32] = return_ref[...]
    packed = pad[...]
    by40 = pltpu.roll(packed, 40, axis=1)
    by80 = pltpu.roll(packed, 80, axis=1)
    entry = [
        jnp.where(
            lane1 < 40,
            packed[0:1],
            jnp.where(lane1 < 80, by40[1:2], jnp.where(lane1 < 120, by80[2:3], 3072)),
        ),
        jnp.where(lane1 < 40, packed[3:4], jnp.where(lane1 < 80, by40[4:5], 3072)),
    ]
    direction = [
        jnp.where(lane1 < 40, packed[5:6], jnp.where(lane1 < 80, by40[5:6], by80[5:6])),
        jnp.where(lane1 < 40, packed[5:6], by40[5:6]),
    ]
    by32 = pltpu.roll(packed, 32, axis=1)
    by64 = pltpu.roll(packed, 64, axis=1)
    by96 = pltpu.roll(packed, 96, axis=1)
    leaving = jnp.where(
        lane < 32, packed, jnp.where(lane < 64, by32, jnp.where(lane < 96, by64, by96))
    )[6:8]

    for m in range(2):
        tile, place = placed(entry[m])
        tile, place = wide(tile), wide(place)
        value = rest
        for f in range(4):
            for c in range(TILES):
                value = jnp.where(tile == f * TILES + c, lanes_of(tr[f, c], place), value)
        mor[m] = value

    for p in (3, 7, 2, 6, 1, 5):
        trace_copy(p).start()
    small[4].wait()

    def local_step(c, carry):
        span = pl.ds(pl.multiple_of(128 * c, 128), 128)
        for f in range(6):
            tile, place = placed(partner_ref[f : f + 1, span])
            tile, place = wide(tile), wide(place)
            value = rest
            for t in range(TILES):
                value = jnp.where(
                    tile == (f ^ 1) * TILES + t, lanes_of(tr[f ^ 1, t], place), value
                )
            acc[f, c] = value
        return carry

    lax.fori_loop(0, TILES, local_step, 0)

    trace_copy(0).wait_recv()
    trace_copy(4).wait_recv()
    small[7].wait()
    states = []
    for m in range(2):
        tile, place = placed(entry[m])
        tile, place = wide(tile), wide(place)
        value = mor[m]
        for p in (0, 4):
            value = jnp.where(tile == 24 + p, lanes_of(rcv[p], place), value)
        states.append(value)
    lane80 = wide(lane1)
    big = jnp.where(
        lane80 < 40,
        states[0],
        jnp.where(
            lane80 < 80,
            pltpu.roll(states[0], 40, axis=1),
            pltpu.roll(states[0], 80, axis=1),
        ),
    )
    near = jnp.dot(
        matrix_ref[0:320], big, precision=HIGHEST, preferred_element_type=jnp.float32
    )
    nears = [
        jnp.where(lane80 < 80, near[0:80], near[80:160]),
        jnp.where(lane80 < 40, near[160:240], near[240:320]),
    ]
    stars = []
    for m in range(2):
        normal = [
            wide(
                jnp.where(direction[m] == 2 * axis + 1, 1.0, 0.0)
                - jnp.where(direction[m] == 2 * axis, 1.0, 0.0),
                16,
            )
            for axis in range(3)
        ]
        inside, outside = split(nears[m]), split(states[m])
        inside_flux, inside_speed = normal_flux(inside, normal)
        outside_flux, outside_speed = normal_flux(outside, normal)
        half = 0.5 * jnp.maximum(inside_speed, outside_speed)
        stars.append(
            jnp.concatenate(
                [
                    0.5 * (inside_flux[v] + outside_flux[v]) - half * (outside[v] - inside[v])
                    for v in range(5)
                ],
                axis=0,
            )
        )
    home_a = jnp.dot(
        matrix_ref[320:480], stars[0], precision=HIGHEST, preferred_element_type=jnp.float32
    )
    home_b = jnp.dot(
        matrix_ref[480:640], stars[1], precision=HIGHEST, preferred_element_type=jnp.float32
    )
    together = (
        pltpu.roll(home_a[0:80], 88, axis=1)
        + pltpu.roll(home_a[80:160], 48, axis=1)
        + home_b[0:80]
        + pltpu.roll(home_b[80:160], 88, axis=1)
    )
    tab[0] = jnp.where(lane80 < 40, together, -stars[0])
    tab[1] = -stars[1]

    def return_copy(side):
        step = 1 - 2 * side
        return pltpu.make_async_remote_copy(
            src_ref=rsnd.at[side],
            dst_ref=rrcv.at[side],
            send_sem=rsend_sem.at[side],
            recv_sem=rrecv_sem.at[side],
            device_id=(lax.rem(me + step + count, count),),
            device_id_type=MESH,
        )

    quarter = jnp.right_shift(lane, 5)
    for side in range(2):
        index = wide(leaving[side : side + 1], 8)
        first = index < 120
        named = index < 200
        place = jnp.bitwise_and(jnp.where(first, index, index - 120), 127)
        for k in range(3):
            value = jnp.zeros((8, 128), jnp.float32)
            for b in range(4):
                g = 4 * k + b
                if g < 10:
                    rows = slice(8 * g, 8 * g + 8)
                    found = jnp.where(
                        first, lanes_of(tab[0, rows], place), lanes_of(tab[1, rows], place)
                    )
                    value = jnp.where((quarter == b) & named, found, value)
            rsnd[side, 8 * k : 8 * k + 8] = value
        return_copy(side).start()

    small[5].wait()

    def hang_step(c, carry):
        span = pl.ds(pl.multiple_of(128 * c, 128), 128)
        for f in range(4):
            index = wide(source_ref[f : f + 1, span])
            first = index < 120
            place = jnp.bitwise_and(jnp.where(first, index, index - 120), 127)
            found = jnp.where(first, lanes_of(tab[0], place), lanes_of(tab[1], place))
            hang[f, c] = jnp.where(index < 200, found - own[f, c], 0.0)
        return carry

    lax.fori_loop(0, TILES, hang_step, 0)

    def arrive_step(k, carry):
        p = lax.rem(4 - k, 4)

        @pl.when(k >= 1)
        def _():
            trace_copy(p).wait_recv()
            trace_copy(p + 4).wait_recv()

        for c in range(TILES):
            for f in range(6):
                tile, place = placed(partner_ref[f : f + 1, 128 * c : 128 * c + 128])
                tile, place = wide(tile), wide(place)
                value = acc[f, c]
                for q in (p, p + 4):
                    value = jnp.where(tile == 24 + q, lanes_of(rcv[q], place), value)
                acc[f, c] = value
        return carry

    lax.fori_loop(0, 4, arrive_step, 0)
    small[6].wait()

    for c in range(TILES):
        span = slice(128 * c, 128 * c + 128)
        ends = [[None] * 5, [None] * 5]
        for f in range(6):
            here, there = tr[f, c], acc[f, c]
            inside, outside = split(here), split(there)
            flux, speed = axis_flux(outside, SIDE[f], 2.0 * (f % 2) - 1.0)
            half = 0.5 * jnp.maximum(spd[f, c], speed)
            jumps = [
                0.5 * (flux[v] - own[f, c, 16 * v : 16 * v + 16]) - half * (outside[v] - inside[v])
                for v in range(5)
            ]
            if f < 4:
                plain = wide(source_ref[f : f + 1, span], 16) == 200
                for v in range(5):
                    jumps[v] = jnp.where(plain, jumps[v], hang[f, c, 16 * v : 16 * v + 16])
            for v in range(5):
                if f < 2:
                    ends[f][v] = jumps[v]
                elif f < 4:
                    for i in range(4):
                        at = 16 * i + 12 * (f - 2)
                        lift_j[c, v, at : at + 4] = jumps[v][4 * i : 4 * i + 4]
                else:
                    lift_k[c, v, pl.ds(3 * (f - 4), 16, 4)] = jumps[v]
        for v in range(5):
            for i in range(4):
                rows = slice(16 * i, 16 * i + 16)
                lift = lift_j[c, v, rows] + lift_k[c, v, rows]
                if i in (0, 3):
                    lift += ends[i // 3][v]
                res[c, v, rows] += 6.0 * lift

    return_copy(0).wait_recv()
    return_copy(1).wait_recv()
    for p in range(8):
        trace_copy(p).wait_send()
    for side in range(2):
        return_copy(side).wait_send()


def close_kernel(
    res,
    own,
    rrcv,
    source_ref,
    levels_ref,
    step_ref,
    out_hbm,
    done,
    lift_j,
    out_sem,
):
    def wide(row, rows):
        return jnp.broadcast_to(row, (rows, 128))

    copies = []
    for v in range(5):
        lift_j[v] = jnp.zeros((64, 128), jnp.float32)
    for c in range(TILES):
        span = slice(128 * c, 128 * c + 128)
        ends = [[None] * 5, [None] * 5]
        for f in range(4):
            index = wide(source_ref[f : f + 1, span], 8)
            near_side, named = index < 233, index > 200
            back = jnp.bitwise_and(jnp.where(near_side, index - 201, index - 233), 31)
            backs = [back + 32 * b for b in range(4)]
            for v in range(5):
                pieces = []
                for g in (2 * v, 2 * v + 1):
                    packs = slice(8 * (g // 4), 8 * (g // 4) + 8)
                    far = backs[g % 4]
                    came = jnp.where(
                        near_side,
                        lanes_of(rrcv[0, packs], far),
                        lanes_of(rrcv[1, packs], far),
                    )
                    pieces.append(
                        jnp.where(named, came - own[f, c, 8 * g : 8 * g + 8], 0.0)
                    )
                if f < 2:
                    ends[f][v] = jnp.concatenate(pieces, axis=0)
                else:
                    for i in range(4):
                        at = 16 * i + 12 * (f - 2)
                        half_rows = slice(4 * (i % 2), 4 * (i % 2) + 4)
                        lift_j[v, at : at + 4] = pieces[i // 2][half_rows]
        scale = -step_ref[0] * jnp.exp2(levels_ref[0:1, span].astype(jnp.float32) + 1.0)
        for v in range(5):
            for i in range(4):
                rows = slice(16 * i, 16 * i + 16)
                lift = lift_j[v, rows]
                if i in (0, 3):
                    lift += ends[i // 3][v]
                done[c, v, rows] = wide(scale, 16) * (res[c, v, rows] + 6.0 * lift)
        copies.append(
            pltpu.make_async_copy(done.at[c], out_hbm.at[:, :, span], out_sem.at[c])
        )
        copies[c].start()
    for copy in copies:
        copy.wait()


def body(
    state, step_size, levels, send_faces, partner, mortar_in, mortar_dir, return_faces, flux_source
):


    count = lax.axis_size("dev")
    vmem = pl.BlockSpec(memory_space=pltpu.VMEM)
    f32 = jnp.float32
    kept = (
        pltpu.VMEM((TILES, 5, 64, 128), f32),
        pltpu.VMEM((6, TILES, 80, 128), f32),
        pltpu.VMEM((2, 24, 128), f32),
        pltpu.VMEM((6, 512), jnp.int32),
        pltpu.VMEM((1, 512), jnp.int32),
    )
    parts = pl.pallas_call(
        functools.partial(kernel, count),
        out_shape=kept,
        in_specs=[pl.BlockSpec(memory_space=pltpu.HBM)] * 9,
        out_specs=(vmem,) * 5,
        scratch_shapes=[
            pltpu.VMEM((8, 128), jnp.int32),
            pltpu.VMEM((6, 512), jnp.int32),
            pltpu.VMEM((5, 40), jnp.int32),
            pltpu.VMEM((1, 40), jnp.int32),
            pltpu.VMEM((2, 32), jnp.int32),
            pltpu.VMEM((640, 80), f32),
            pltpu.VMEM((TILES, 5, 64, 128), f32),
            pltpu.VMEM((6, TILES, 80, 128), f32),
            pltpu.VMEM((8, 80, 128), f32),
            pltpu.VMEM((8, 80, 128), f32),
            pltpu.VMEM((6, TILES, 80, 128), f32),
            pltpu.VMEM((6, TILES, 16, 128), f32),
            pltpu.VMEM((2, 5, 64, 128), f32),
            pltpu.VMEM((2, 80, 128), f32),
            pltpu.VMEM((2, 80, 128), f32),
            pltpu.VMEM((2, 24, 128), f32),
            pltpu.VMEM((8, 128), jnp.int32),
            pltpu.VMEM((4, TILES, 80, 128), f32),
            pltpu.VMEM((TILES, 5, 64, 128), f32),
            pltpu.VMEM((TILES, 5, 64, 128), f32),
            pltpu.SemaphoreType.DMA((TILES,)),
            pltpu.SemaphoreType.DMA((8,)),
            pltpu.SemaphoreType.DMA((8,)),
            pltpu.SemaphoreType.DMA((8,)),
            pltpu.SemaphoreType.DMA((2,)),
            pltpu.SemaphoreType.DMA((2,)),
        ],
        compiler_params=pltpu.CompilerParams(
            collective_id=0, has_side_effects=True, vmem_limit_bytes=24 * 1024 * 1024
        ),
        name="section",
    )(
        *(
            pltpu.with_memory_space_constraint(array, pltpu.HBM)
            for array in (
                state,
                levels.reshape(1, -1),
                send_faces,
                partner,
                mortar_in,
                mortar_dir.reshape(1, -1),
                return_faces,
                flux_source,
                jnp.asarray(mortar_matrices()),
            )
        )
    )
    return pl.pallas_call(
        close_kernel,
        out_shape=jax.ShapeDtypeStruct(state.shape, f32),
        in_specs=[vmem] * 5 + [pl.BlockSpec(memory_space=pltpu.SMEM)],
        out_specs=pl.BlockSpec(memory_space=pltpu.HBM),
        scratch_shapes=[
            pltpu.VMEM((TILES, 5, 64, 128), f32),
            pltpu.VMEM((5, 64, 128), f32),
            pltpu.SemaphoreType.DMA((TILES,)),
        ],
        compiler_params=pltpu.CompilerParams(vmem_limit_bytes=8 * 1024 * 1024),
        name="close",
    )(*(pltpu.with_memory_space_constraint(part, pltpu.VMEM) for part in parts), step_size)


def solution(mesh):
    placed = (
        P(None, None, "dev"),
        P(),
        P("dev"),
        P("dev", None),
        P(None, "dev"),
        P(None, "dev"),
        P("dev"),
        P("dev", None),
        P(None, "dev"),
    )
    return jax.shard_map(
        body, mesh=mesh, in_specs=placed, out_specs=P(None, None, "dev"), check_vma=False
    )
```

```python
import functools

import jax
import jax.numpy as jnp
import ml_dtypes
import numpy as np
from jax import lax
from jax.experimental import pallas as pl
from jax.experimental.pallas import tpu as pltpu
from jax.sharding import PartitionSpec as P

GAMMA = 1.4
MESH = pl.DeviceIdType.MESH
TILES = 4
SIDE = (0, 0, 1, 1, 2, 2)


def lobatto_tables():
    nodes = np.array([-1.0, -1.0 / np.sqrt(5.0), 1.0 / np.sqrt(5.0), 1.0])
    weights = np.array([1.0, 5.0, 5.0, 1.0]) / 6.0

    def basis(points):
        table = np.ones((len(points), 4))
        for column in range(4):
            for other in range(4):
                if other != column:
                    table[:, column] *= (points - nodes[other]) / (nodes[column] - nodes[other])
        return table

    derivative = np.zeros((4, 4))
    for row in range(4):
        for column in range(4):
            total = 0.0
            for other in range(4):
                if other != column:
                    term = 1.0 / (nodes[column] - nodes[other])
                    for third in range(4):
                        if third != column and third != other:
                            term *= (nodes[row] - nodes[third]) / (nodes[column] - nodes[third])
                    total += term
            derivative[row, column] = total
    lower = basis((nodes - 1.0) / 2.0)
    upper = basis((nodes + 1.0) / 2.0)
    back_lower = 0.5 * (lower.T * weights[None, :]) / weights[:, None]
    back_upper = 0.5 * (upper.T * weights[None, :]) / weights[:, None]
    return [
        np.asarray(table, np.float32)
        for table in (derivative, lower, upper, back_lower, back_upper)
    ]


def mortar_matrices():
    _, lower, upper, back_lower, back_upper = [t.astype(np.float64) for t in lobatto_tables()]
    ahead, back = (lower, upper), (back_lower, back_upper)
    five = np.eye(5)
    forth = [np.kron(five, np.kron(ahead[q % 2], ahead[q // 2])) for q in range(4)]
    home = [np.kron(five, np.kron(back[q % 2], back[q // 2])) for q in range(4)]
    whole = np.concatenate(forth + home, axis=0)
    upper_part = whole.astype(ml_dtypes.bfloat16)
    lower_part = (whole - upper_part.astype(np.float64)).astype(ml_dtypes.bfloat16)
    return np.concatenate([upper_part, upper_part, lower_part], axis=1)


def product(matrix, columns):
    coarse = columns.astype(jnp.bfloat16)
    rest = (columns - coarse.astype(jnp.float32)).astype(jnp.bfloat16)
    stacked = jnp.concatenate([coarse, rest, coarse], axis=0)
    return jnp.dot(matrix, stacked, preferred_element_type=jnp.float32)


def lanes_of(tile, index):
    return jnp.take_along_axis(tile, index, axis=1, mode="promise_in_bounds")


def axis_flux(parts, axis, sign):
    density, energy = parts[0], parts[4]
    inverse = 1.0 / density
    along = sign * parts[1 + axis] * inverse
    kinetic = parts[1] * parts[1] + parts[2] * parts[2] + parts[3] * parts[3]
    pressure = (GAMMA - 1.0) * (energy - 0.5 * kinetic * inverse)
    flux = [density * along]
    for other in range(3):
        term = parts[1 + other] * along
        flux.append(term + sign * pressure if other == axis else term)
    flux.append((energy + pressure) * along)
    speed = jnp.abs(along) + jnp.sqrt(GAMMA * pressure * inverse)
    return flux, speed


def normal_flux(parts, normal):
    density, energy = parts[0], parts[4]
    motion = [parts[1 + axis] / density for axis in range(3)]
    pressure = (GAMMA - 1.0) * (
        energy - 0.5 * (parts[1] * motion[0] + parts[2] * motion[1] + parts[3] * motion[2])
    )
    along = motion[0] * normal[0] + motion[1] * normal[1] + motion[2] * normal[2]
    flux = [density * along]
    for axis in range(3):
        flux.append(parts[1 + axis] * along + pressure * normal[axis])
    flux.append((energy + pressure) * along)
    speed = jnp.abs(along) + jnp.sqrt(GAMMA * pressure / density)
    return flux, speed


def split(columns):
    return [columns[16 * v : 16 * v + 16] for v in range(5)]


def rest_state():
    row = lax.broadcasted_iota(jnp.int32, (80, 128), 0)
    return jnp.where(row < 16, 1.0, jnp.where(row >= 64, 2.5, 0.0)).astype(jnp.float32)


def kernel(
    count,
    state_hbm,
    levels_hbm,
    send_hbm,
    partner_hbm,
    mortar_hbm,
    dir_hbm,
    return_hbm,
    source_hbm,
    matrix_hbm,
    res,
    own,
    rrcv,
    source_ref,
    levels_ref,
    send_ref,
    partner_ref,
    mortar_ref,
    dir_ref,
    return_ref,
    matrix_ref,
    st,
    tr,
    snd,
    rcv,
    acc,
    spd,
    ftmp,
    mor,
    tab,
    rsnd,
    pad,
    hang,
    lift_j,
    lift_k,
    load_sem,
    small_sem,
    send_sem,
    recv_sem,
    rsend_sem,
    rrecv_sem,
):
    me = lax.axis_index("dev")
    derivative = [[float(x) for x in row] for row in lobatto_tables()[0]]

    def peer_of(p):
        offset = jnp.where(p < 4, p + 1, 3 - p)
        return lax.rem(me + offset + count, count)

    barrier = pltpu.get_barrier_semaphore()
    for p in range(8):
        pl.semaphore_signal(barrier, inc=1, device_id=(peer_of(p),), device_id_type=MESH)

    def load_of(c):
        span = pl.ds(pl.multiple_of(128 * c, 128), 128)
        return pltpu.make_async_copy(state_hbm.at[:, :, span], st.at[c], load_sem.at[c])

    for c in range(TILES):
        load_of(c).start()
    small = [
        pltpu.make_async_copy(source, target, small_sem.at[n])
        for n, (source, target) in enumerate(
            (
                (send_hbm, send_ref),
                (mortar_hbm, mortar_ref),
                (dir_hbm, dir_ref),
                (return_hbm, return_ref),
                (partner_hbm, partner_ref),
                (source_hbm, source_ref),
                (levels_hbm, levels_ref),
                (matrix_hbm, matrix_ref),
            )
        )
    ]
    for load in small:
        load.start()

    lane = lax.broadcasted_iota(jnp.int32, (8, 128), 1)
    lane1 = lane[0:1]
    rest = rest_state()

    def placed(index):
        moved = jnp.where(index > 3072, index - 1, index)
        tile = jnp.where(index == 3072, -1, jnp.right_shift(moved, 7))
        return tile, jnp.bitwise_and(moved, 127)

    def wide(row, rows=80):
        return jnp.broadcast_to(row, (rows, 128))

    def trace_step(c, carry):
        load_of(c).wait()
        for v in range(5):
            tr[0, c, 16 * v : 16 * v + 16] = st[c, v, 0:16]
            tr[1, c, 16 * v : 16 * v + 16] = st[c, v, 48:64]
            for i in range(4):
                tr[2, c, 16 * v + 4 * i : 16 * v + 4 * i + 4] = st[c, v, 16 * i : 16 * i + 4]
                tr[3, c, 16 * v + 4 * i : 16 * v + 4 * i + 4] = st[c, v, 16 * i + 12 : 16 * i + 16]
            tr[4, c, 16 * v : 16 * v + 16] = st[c, v, pl.ds(0, 16, 4)]
            tr[5, c, 16 * v : 16 * v + 16] = st[c, v, pl.ds(3, 16, 4)]
        return carry

    lax.fori_loop(0, TILES, trace_step, 0)


    def trace_copy(p):
        return pltpu.make_async_remote_copy(
            src_ref=snd.at[p],
            dst_ref=rcv.at[p],
            send_sem=send_sem.at[p],
            recv_sem=recv_sem.at[p],
            device_id=(peer_of(p),),
            device_id_type=MESH,
        )

    def order(k):
        return lax.rem(k, 2) * 4 + lax.rem(4 - k // 2, 4)

    row16 = lax.broadcasted_iota(jnp.int32, (16, 128), 0)
    second = jnp.right_shift(row16, 2)

    def by_row(shift):
        picks = [derivative[j][(j - shift) % 4] for j in range(4)]
        return jnp.where(
            second == 0,
            picks[0],
            jnp.where(second == 1, picks[1], jnp.where(second == 2, picks[2], picks[3])),
        ).astype(jnp.float32)

    weights = [by_row(shift) for shift in range(4)]

    def fluxes_of(c):
        for i in range(4):
            rows = pl.ds(16 * i, 16)
            parts = [st[c, v, rows] for v in range(5)]
            inverse = 1.0 / parts[0]
            motion = [parts[1 + a] * inverse for a in range(3)]
            pressure = (GAMMA - 1.0) * (
                parts[4]
                - 0.5 * (parts[1] * motion[0] + parts[2] * motion[1] + parts[3] * motion[2])
            )
            for axis in range(3):
                flux = [parts[1 + axis]]
                for other in range(3):
                    term = parts[1 + other] * motion[axis]
                    flux.append(term + pressure if other == axis else term)
                flux.append((parts[4] + pressure) * motion[axis])
                for v in range(5):
                    if axis == 0:
                        ftmp[0, v, rows] = flux[v]
                    elif axis == 2:
                        ftmp[1, v, rows] = flux[v]
                    else:
                        total = weights[0] * flux[v]
                        for shift in range(1, 4):
                            total += weights[shift] * pltpu.roll(flux[v], 4 * shift, axis=0)
                        res[c, v, rows] = total

    def slopes_of(c):
        for v in range(5):
            terms = [ftmp[0, v, 16 * i : 16 * i + 16] for i in range(4)]
            for a in range(4):
                total = res[c, v, 16 * a : 16 * a + 16]
                for i in range(4):
                    total += derivative[a][i] * terms[i]
                res[c, v, 16 * a : 16 * a + 16] = total
        for v in range(5):
            terms = [ftmp[1, v, pl.ds(k, 16, 4)] for k in range(4)]
            for a in range(4):
                total = res[c, v, pl.ds(a, 16, 4)]
                for k in range(4):
                    total += derivative[a][k] * terms[k]
                res[c, v, pl.ds(a, 16, 4)] = total

    def own_fluxes_of(c):
        for f in range(6):
            flux, speed = axis_flux(split(tr[f, c]), SIDE[f], 2.0 * (f % 2) - 1.0)
            for v in range(5):
                own[f, c, 16 * v : 16 * v + 16] = flux[v]
            spd[f, c] = speed

    def outgoing(p):
        index = send_ref[pl.ds(p, 1), :]
        tile = wide(jnp.right_shift(index, 7))
        place = wide(jnp.bitwise_and(index, 127))
        value = rest
        for f in range(6):
            for c in range(TILES):
                value = jnp.where(tile == f * TILES + c, lanes_of(tr[f, c], place), value)
        snd[p] = value

    def send_step(c, carry):
        p = lax.rem(4 - c, 4)
        outgoing(p)
        outgoing(p + 4)
        return carry

    small[0].wait()
    lax.fori_loop(0, TILES, send_step, 0)
    pl.semaphore_wait(barrier, 8)
    for p in (4, 0):
        trace_copy(p).start()

    for n in (1, 2, 3):
        small[n].wait()
    pad[...] = jnp.full((8, 128), 3072, jnp.int32)
    pad[0:5, 0:40] = mortar_ref[...]
    pad[5:6, 0:40] = dir_ref[...]
    pad[6:8, 0:32] = return_ref[...]
    packed = pad[...]
    by40 = pltpu.roll(packed, 40, axis=1)
    by80 = pltpu.roll(packed, 80, axis=1)
    entry = [
        jnp.where(
            lane1 < 40,
            packed[0:1],
            jnp.where(lane1 < 80, by40[1:2], jnp.where(lane1 < 120, by80[2:3], 3072)),
        ),
        jnp.where(lane1 < 40, packed[3:4], jnp.where(lane1 < 80, by40[4:5], 3072)),
    ]
    direction = [
        jnp.where(lane1 < 40, packed[5:6], jnp.where(lane1 < 80, by40[5:6], by80[5:6])),
        jnp.where(lane1 < 40, packed[5:6], by40[5:6]),
    ]
    by32 = pltpu.roll(packed, 32, axis=1)
    by64 = pltpu.roll(packed, 64, axis=1)
    by96 = pltpu.roll(packed, 96, axis=1)
    leaving = jnp.where(
        lane < 32, packed, jnp.where(lane < 64, by32, jnp.where(lane < 96, by64, by96))
    )[6:8]

    for m in range(2):
        tile, place = placed(entry[m])
        tile, place = wide(tile), wide(place)
        value = rest
        for f in range(4):
            for c in range(TILES):
                value = jnp.where(tile == f * TILES + c, lanes_of(tr[f, c], place), value)
        mor[m] = value

    for p in (3, 7, 2, 6, 1, 5):
        trace_copy(p).start()
    small[4].wait()

    def local_step(c, carry):
        fluxes_of(c)
        slopes_of(c)
        own_fluxes_of(c)
        for v in range(5):
            lift_j[c, v] = jnp.zeros((64, 128), jnp.float32)
            lift_k[c, v] = jnp.zeros((64, 128), jnp.float32)
        span = pl.ds(pl.multiple_of(128 * c, 128), 128)
        for f in range(6):
            tile, place = placed(partner_ref[f : f + 1, span])
            tile, place = wide(tile), wide(place)
            value = rest
            for t in range(TILES):
                value = jnp.where(
                    tile == (f ^ 1) * TILES + t, lanes_of(tr[f ^ 1, t], place), value
                )
            acc[f, c] = value
        return carry

    lax.fori_loop(0, TILES, local_step, 0)

    trace_copy(0).wait_recv()
    trace_copy(4).wait_recv()
    small[7].wait()
    states = []
    for m in range(2):
        tile, place = placed(entry[m])
        tile, place = wide(tile), wide(place)
        value = mor[m]
        for p in (0, 4):
            value = jnp.where(tile == 24 + p, lanes_of(rcv[p], place), value)
        states.append(value)
    lane80 = wide(lane1)
    big = jnp.where(
        lane80 < 40,
        states[0],
        jnp.where(
            lane80 < 80,
            pltpu.roll(states[0], 40, axis=1),
            pltpu.roll(states[0], 80, axis=1),
        ),
    )
    near = product(matrix_ref[0:320], big)
    nears = [
        jnp.where(lane80 < 80, near[0:80], near[80:160]),
        jnp.where(lane80 < 40, near[160:240], near[240:320]),
    ]
    stars = []
    for m in range(2):
        normal = [
            wide(
                jnp.where(direction[m] == 2 * axis + 1, 1.0, 0.0)
                - jnp.where(direction[m] == 2 * axis, 1.0, 0.0),
                16,
            )
            for axis in range(3)
        ]
        inside, outside = split(nears[m]), split(states[m])
        inside_flux, inside_speed = normal_flux(inside, normal)
        outside_flux, outside_speed = normal_flux(outside, normal)
        half = 0.5 * jnp.maximum(inside_speed, outside_speed)
        stars.append(
            jnp.concatenate(
                [
                    0.5 * (inside_flux[v] + outside_flux[v]) - half * (outside[v] - inside[v])
                    for v in range(5)
                ],
                axis=0,
            )
        )
    home_a = product(matrix_ref[320:480], stars[0])
    home_b = product(matrix_ref[480:640], stars[1])
    together = (
        pltpu.roll(home_a[0:80], 88, axis=1)
        + pltpu.roll(home_a[80:160], 48, axis=1)
        + home_b[0:80]
        + pltpu.roll(home_b[80:160], 88, axis=1)
    )
    tab[0] = jnp.where(lane80 < 40, together, -stars[0])
    tab[1] = -stars[1]

    def return_copy(side):
        step = 1 - 2 * side
        return pltpu.make_async_remote_copy(
            src_ref=rsnd.at[side],
            dst_ref=rrcv.at[side],
            send_sem=rsend_sem.at[side],
            recv_sem=rrecv_sem.at[side],
            device_id=(lax.rem(me + step + count, count),),
            device_id_type=MESH,
        )

    quarter = jnp.right_shift(lane, 5)
    for side in range(2):
        index = wide(leaving[side : side + 1], 8)
        first = index < 120
        named = index < 200
        place = jnp.bitwise_and(jnp.where(first, index, index - 120), 127)
        for k in range(3):
            value = jnp.zeros((8, 128), jnp.float32)
            for b in range(4):
                g = 4 * k + b
                if g < 10:
                    rows = slice(8 * g, 8 * g + 8)
                    found = jnp.where(
                        first, lanes_of(tab[0, rows], place), lanes_of(tab[1, rows], place)
                    )
                    value = jnp.where((quarter == b) & named, found, value)
            rsnd[side, 8 * k : 8 * k + 8] = value
        return_copy(side).start()

    small[5].wait()

    def hang_step(c, carry):
        span = pl.ds(pl.multiple_of(128 * c, 128), 128)
        for f in range(4):
            index = wide(source_ref[f : f + 1, span])
            first = index < 120
            place = jnp.bitwise_and(jnp.where(first, index, index - 120), 127)
            found = jnp.where(first, lanes_of(tab[0], place), lanes_of(tab[1], place))
            hang[f, c] = jnp.where(index < 200, found - own[f, c], 0.0)
        return carry

    lax.fori_loop(0, TILES, hang_step, 0)

    def arrive_step(k, carry):
        p = lax.rem(4 - k, 4)

        @pl.when(k >= 1)
        def _():
            trace_copy(p).wait_recv()
            trace_copy(p + 4).wait_recv()

        for c in range(TILES):
            for f in range(6):
                tile, place = placed(partner_ref[f : f + 1, 128 * c : 128 * c + 128])
                tile, place = wide(tile), wide(place)
                value = acc[f, c]
                for q in (p, p + 4):
                    value = jnp.where(tile == 24 + q, lanes_of(rcv[q], place), value)
                acc[f, c] = value
        return carry

    lax.fori_loop(0, 4, arrive_step, 0)
    small[6].wait()

    for c in range(TILES):
        span = slice(128 * c, 128 * c + 128)
        ends = [[None] * 5, [None] * 5]
        for f in range(6):
            here, there = tr[f, c], acc[f, c]
            inside, outside = split(here), split(there)
            flux, speed = axis_flux(outside, SIDE[f], 2.0 * (f % 2) - 1.0)
            half = 0.5 * jnp.maximum(spd[f, c], speed)
            jumps = [
                0.5 * (flux[v] - own[f, c, 16 * v : 16 * v + 16]) - half * (outside[v] - inside[v])
                for v in range(5)
            ]
            if f < 4:
                plain = wide(source_ref[f : f + 1, span], 16) == 200
                for v in range(5):
                    jumps[v] = jnp.where(plain, jumps[v], hang[f, c, 16 * v : 16 * v + 16])
            for v in range(5):
                if f < 2:
                    ends[f][v] = jumps[v]
                elif f < 4:
                    for i in range(4):
                        at = 16 * i + 12 * (f - 2)
                        lift_j[c, v, at : at + 4] = jumps[v][4 * i : 4 * i + 4]
                else:
                    lift_k[c, v, pl.ds(3 * (f - 4), 16, 4)] = jumps[v]
        for v in range(5):
            for i in range(4):
                rows = slice(16 * i, 16 * i + 16)
                lift = lift_j[c, v, rows] + lift_k[c, v, rows]
                if i in (0, 3):
                    lift += ends[i // 3][v]
                res[c, v, rows] += 6.0 * lift

    return_copy(0).wait_recv()
    return_copy(1).wait_recv()
    for p in range(8):
        trace_copy(p).wait_send()
    for side in range(2):
        return_copy(side).wait_send()


def close_kernel(
    res,
    own,
    rrcv,
    source_ref,
    levels_ref,
    step_ref,
    out_hbm,
    done,
    lift_j,
    out_sem,
):
    def wide(row, rows):
        return jnp.broadcast_to(row, (rows, 128))

    copies = []
    for v in range(5):
        lift_j[v] = jnp.zeros((64, 128), jnp.float32)
    for c in range(TILES):
        span = slice(128 * c, 128 * c + 128)
        ends = [[None] * 5, [None] * 5]
        for f in range(4):
            index = wide(source_ref[f : f + 1, span], 8)
            near_side, named = index < 233, index > 200
            back = jnp.bitwise_and(jnp.where(near_side, index - 201, index - 233), 31)
            backs = [back + 32 * b for b in range(4)]
            for v in range(5):
                pieces = []
                for g in (2 * v, 2 * v + 1):
                    packs = slice(8 * (g // 4), 8 * (g // 4) + 8)
                    far = backs[g % 4]
                    came = jnp.where(
                        near_side,
                        lanes_of(rrcv[0, packs], far),
                        lanes_of(rrcv[1, packs], far),
                    )
                    pieces.append(
                        jnp.where(named, came - own[f, c, 8 * g : 8 * g + 8], 0.0)
                    )
                if f < 2:
                    ends[f][v] = jnp.concatenate(pieces, axis=0)
                else:
                    for i in range(4):
                        at = 16 * i + 12 * (f - 2)
                        half_rows = slice(4 * (i % 2), 4 * (i % 2) + 4)
                        lift_j[v, at : at + 4] = pieces[i // 2][half_rows]
        scale = -step_ref[0] * jnp.exp2(levels_ref[0:1, span].astype(jnp.float32) + 1.0)
        for v in range(5):
            for i in range(4):
                rows = slice(16 * i, 16 * i + 16)
                lift = lift_j[v, rows]
                if i in (0, 3):
                    lift += ends[i // 3][v]
                done[c, v, rows] = wide(scale, 16) * (res[c, v, rows] + 6.0 * lift)
        copies.append(
            pltpu.make_async_copy(done.at[c], out_hbm.at[:, :, span], out_sem.at[c])
        )
        copies[c].start()
    for copy in copies:
        copy.wait()


def body(
    state, step_size, levels, send_faces, partner, mortar_in, mortar_dir, return_faces, flux_source
):


    count = lax.axis_size("dev")
    vmem = pl.BlockSpec(memory_space=pltpu.VMEM)
    f32 = jnp.float32
    kept = (
        pltpu.VMEM((TILES, 5, 64, 128), f32),
        pltpu.VMEM((6, TILES, 80, 128), f32),
        pltpu.VMEM((2, 24, 128), f32),
        pltpu.VMEM((6, 512), jnp.int32),
        pltpu.VMEM((1, 512), jnp.int32),
    )
    parts = pl.pallas_call(
        functools.partial(kernel, count),
        out_shape=kept,
        in_specs=[pl.BlockSpec(memory_space=pltpu.HBM)] * 9,
        out_specs=(vmem,) * 5,
        scratch_shapes=[
            pltpu.VMEM((8, 128), jnp.int32),
            pltpu.VMEM((6, 512), jnp.int32),
            pltpu.VMEM((5, 40), jnp.int32),
            pltpu.VMEM((1, 40), jnp.int32),
            pltpu.VMEM((2, 32), jnp.int32),
            pltpu.VMEM((640, 240), jnp.bfloat16),
            pltpu.VMEM((TILES, 5, 64, 128), f32),
            pltpu.VMEM((6, TILES, 80, 128), f32),
            pltpu.VMEM((8, 80, 128), f32),
            pltpu.VMEM((8, 80, 128), f32),
            pltpu.VMEM((6, TILES, 80, 128), f32),
            pltpu.VMEM((6, TILES, 16, 128), f32),
            pltpu.VMEM((2, 5, 64, 128), f32),
            pltpu.VMEM((2, 80, 128), f32),
            pltpu.VMEM((2, 80, 128), f32),
            pltpu.VMEM((2, 24, 128), f32),
            pltpu.VMEM((8, 128), jnp.int32),
            pltpu.VMEM((4, TILES, 80, 128), f32),
            pltpu.VMEM((TILES, 5, 64, 128), f32),
            pltpu.VMEM((TILES, 5, 64, 128), f32),
            pltpu.SemaphoreType.DMA((TILES,)),
            pltpu.SemaphoreType.DMA((8,)),
            pltpu.SemaphoreType.DMA((8,)),
            pltpu.SemaphoreType.DMA((8,)),
            pltpu.SemaphoreType.DMA((2,)),
            pltpu.SemaphoreType.DMA((2,)),
        ],
        compiler_params=pltpu.CompilerParams(
            collective_id=0, has_side_effects=True, vmem_limit_bytes=24 * 1024 * 1024
        ),
        name="section",
    )(
        *(
            pltpu.with_memory_space_constraint(array, pltpu.HBM)
            for array in (
                state,
                levels.reshape(1, -1),
                send_faces,
                partner,
                mortar_in,
                mortar_dir.reshape(1, -1),
                return_faces,
                flux_source,
                jnp.asarray(mortar_matrices()),
            )
        )
    )
    return pl.pallas_call(
        close_kernel,
        out_shape=jax.ShapeDtypeStruct(state.shape, f32),
        in_specs=[vmem] * 5 + [pl.BlockSpec(memory_space=pltpu.SMEM)],
        out_specs=pl.BlockSpec(memory_space=pltpu.HBM),
        scratch_shapes=[
            pltpu.VMEM((TILES, 5, 64, 128), f32),
            pltpu.VMEM((5, 64, 128), f32),
            pltpu.SemaphoreType.DMA((TILES,)),
        ],
        compiler_params=pltpu.CompilerParams(vmem_limit_bytes=8 * 1024 * 1024),
        name="close",
    )(*(pltpu.with_memory_space_constraint(part, pltpu.VMEM) for part in parts), step_size)


def solution(mesh):
    placed = (
        P(None, None, "dev"),
        P(),
        P("dev"),
        P("dev", None),
        P(None, "dev"),
        P(None, "dev"),
        P("dev"),
        P("dev", None),
        P(None, "dev"),
    )
    return jax.shard_map(
        body, mesh=mesh, in_specs=placed, out_specs=P(None, None, "dev"), check_vma=False
    )
```

```python
import functools

import jax
import jax.numpy as jnp
import ml_dtypes
import numpy as np
from jax import lax
from jax.experimental import pallas as pl
from jax.experimental.pallas import tpu as pltpu
from jax.sharding import PartitionSpec as P

GAMMA = 1.4
MESH = pl.DeviceIdType.MESH
TILES = 4
SIDE = (0, 0, 1, 1, 2, 2)


def lobatto_tables():
    nodes = np.array([-1.0, -1.0 / np.sqrt(5.0), 1.0 / np.sqrt(5.0), 1.0])
    weights = np.array([1.0, 5.0, 5.0, 1.0]) / 6.0

    def basis(points):
        table = np.ones((len(points), 4))
        for column in range(4):
            for other in range(4):
                if other != column:
                    table[:, column] *= (points - nodes[other]) / (nodes[column] - nodes[other])
        return table

    derivative = np.zeros((4, 4))
    for row in range(4):
        for column in range(4):
            total = 0.0
            for other in range(4):
                if other != column:
                    term = 1.0 / (nodes[column] - nodes[other])
                    for third in range(4):
                        if third != column and third != other:
                            term *= (nodes[row] - nodes[third]) / (nodes[column] - nodes[third])
                    total += term
            derivative[row, column] = total
    lower = basis((nodes - 1.0) / 2.0)
    upper = basis((nodes + 1.0) / 2.0)
    back_lower = 0.5 * (lower.T * weights[None, :]) / weights[:, None]
    back_upper = 0.5 * (upper.T * weights[None, :]) / weights[:, None]
    return [
        np.asarray(table, np.float32)
        for table in (derivative, lower, upper, back_lower, back_upper)
    ]


def mortar_matrices():
    _, lower, upper, back_lower, back_upper = [t.astype(np.float64) for t in lobatto_tables()]
    ahead, back = (lower, upper), (back_lower, back_upper)
    five = np.eye(5)
    forth = [np.kron(five, np.kron(ahead[q % 2], ahead[q // 2])) for q in range(4)]
    home = [np.kron(five, np.kron(back[q % 2], back[q // 2])) for q in range(4)]
    whole = np.concatenate(forth + home, axis=0)
    upper_part = whole.astype(ml_dtypes.bfloat16)
    lower_part = (whole - upper_part.astype(np.float64)).astype(ml_dtypes.bfloat16)
    return np.concatenate([upper_part, upper_part, lower_part], axis=1)


def product(matrix, columns):
    coarse = columns.astype(jnp.bfloat16)
    rest = (columns - coarse.astype(jnp.float32)).astype(jnp.bfloat16)
    stacked = jnp.concatenate([coarse, rest, coarse], axis=0)
    return jnp.dot(matrix, stacked, preferred_element_type=jnp.float32)


def lanes_of(tile, index):
    return jnp.take_along_axis(tile, index, axis=1, mode="promise_in_bounds")


def axis_flux(parts, axis, sign):
    density, energy = parts[0], parts[4]
    inverse = 1.0 / density
    along = sign * parts[1 + axis] * inverse
    kinetic = parts[1] * parts[1] + parts[2] * parts[2] + parts[3] * parts[3]
    pressure = (GAMMA - 1.0) * (energy - 0.5 * kinetic * inverse)
    flux = [density * along]
    for other in range(3):
        term = parts[1 + other] * along
        flux.append(term + sign * pressure if other == axis else term)
    flux.append((energy + pressure) * along)
    speed = jnp.abs(along) + jnp.sqrt(GAMMA * pressure * inverse)
    return flux, speed


def normal_flux(parts, normal):
    density, energy = parts[0], parts[4]
    motion = [parts[1 + axis] / density for axis in range(3)]
    pressure = (GAMMA - 1.0) * (
        energy - 0.5 * (parts[1] * motion[0] + parts[2] * motion[1] + parts[3] * motion[2])
    )
    along = motion[0] * normal[0] + motion[1] * normal[1] + motion[2] * normal[2]
    flux = [density * along]
    for axis in range(3):
        flux.append(parts[1 + axis] * along + pressure * normal[axis])
    flux.append((energy + pressure) * along)
    speed = jnp.abs(along) + jnp.sqrt(GAMMA * pressure / density)
    return flux, speed


def split(columns):
    return [columns[16 * v : 16 * v + 16] for v in range(5)]


def rest_state():
    row = lax.broadcasted_iota(jnp.int32, (80, 128), 0)
    return jnp.where(row < 16, 1.0, jnp.where(row >= 64, 2.5, 0.0)).astype(jnp.float32)


def kernel(
    count,
    state_hbm,
    levels_hbm,
    send_hbm,
    partner_hbm,
    mortar_hbm,
    dir_hbm,
    return_hbm,
    source_hbm,
    matrix_hbm,
    res,
    own,
    rrcv,
    source_ref,
    levels_ref,
    send_ref,
    partner_ref,
    mortar_ref,
    dir_ref,
    return_ref,
    matrix_ref,
    st,
    tr,
    snd,
    rcv,
    acc,
    spd,
    ftmp,
    mor,
    tab,
    rsnd,
    pad,
    hang,
    lift_j,
    lift_k,
    load_sem,
    small_sem,
    send_sem,
    recv_sem,
    rsend_sem,
    rrecv_sem,
):
    me = lax.axis_index("dev")
    derivative = [[float(x) for x in row] for row in lobatto_tables()[0]]

    def peer_of(p):
        offset = jnp.where(p < 4, p + 1, 3 - p)
        return lax.rem(me + offset + count, count)

    barrier = pltpu.get_barrier_semaphore()
    for p in range(8):
        pl.semaphore_signal(barrier, inc=1, device_id=(peer_of(p),), device_id_type=MESH)

    def load_of(c):
        span = pl.ds(pl.multiple_of(128 * c, 128), 128)
        return pltpu.make_async_copy(state_hbm.at[:, :, span], st.at[c], load_sem.at[c])

    for c in range(TILES):
        load_of(c).start()
    small = [
        pltpu.make_async_copy(source, target, small_sem.at[n])
        for n, (source, target) in enumerate(
            (
                (send_hbm, send_ref),
                (mortar_hbm, mortar_ref),
                (dir_hbm, dir_ref),
                (return_hbm, return_ref),
                (partner_hbm, partner_ref),
                (source_hbm, source_ref),
                (levels_hbm, levels_ref),
                (matrix_hbm, matrix_ref),
            )
        )
    ]
    for load in small:
        load.start()

    lane = lax.broadcasted_iota(jnp.int32, (8, 128), 1)
    lane1 = lane[0:1]
    rest = rest_state()

    def placed(index):
        moved = jnp.where(index > 3072, index - 1, index)
        tile = jnp.where(index == 3072, -1, jnp.right_shift(moved, 7))
        return tile, jnp.bitwise_and(moved, 127)

    def wide(row, rows=80):
        return jnp.broadcast_to(row, (rows, 128))

    def trace_step(c, carry):
        load_of(c).wait()
        for v in range(5):
            tr[0, c, 16 * v : 16 * v + 16] = st[c, v, 0:16]
            tr[1, c, 16 * v : 16 * v + 16] = st[c, v, 48:64]
            for i in range(4):
                tr[2, c, 16 * v + 4 * i : 16 * v + 4 * i + 4] = st[c, v, 16 * i : 16 * i + 4]
                tr[3, c, 16 * v + 4 * i : 16 * v + 4 * i + 4] = st[c, v, 16 * i + 12 : 16 * i + 16]
            tr[4, c, 16 * v : 16 * v + 16] = st[c, v, pl.ds(0, 16, 4)]
            tr[5, c, 16 * v : 16 * v + 16] = st[c, v, pl.ds(3, 16, 4)]
        return carry

    lax.fori_loop(0, TILES, trace_step, 0)


    def trace_copy(p):
        return pltpu.make_async_remote_copy(
            src_ref=snd.at[p],
            dst_ref=rcv.at[p],
            send_sem=send_sem.at[p],
            recv_sem=recv_sem.at[p],
            device_id=(peer_of(p),),
            device_id_type=MESH,
        )

    def order(k):
        return lax.rem(k, 2) * 4 + lax.rem(4 - k // 2, 4)

    row16 = lax.broadcasted_iota(jnp.int32, (16, 128), 0)
    second = jnp.right_shift(row16, 2)

    def by_row(shift):
        picks = [derivative[j][(j - shift) % 4] for j in range(4)]
        return jnp.where(
            second == 0,
            picks[0],
            jnp.where(second == 1, picks[1], jnp.where(second == 2, picks[2], picks[3])),
        ).astype(jnp.float32)

    weights = [by_row(shift) for shift in range(4)]

    def fluxes_of(c):
        for i in range(4):
            rows = pl.ds(16 * i, 16)
            parts = [st[c, v, rows] for v in range(5)]
            inverse = 1.0 / parts[0]
            motion = [parts[1 + a] * inverse for a in range(3)]
            pressure = (GAMMA - 1.0) * (
                parts[4]
                - 0.5 * (parts[1] * motion[0] + parts[2] * motion[1] + parts[3] * motion[2])
            )
            for axis in range(3):
                flux = [parts[1 + axis]]
                for other in range(3):
                    term = parts[1 + other] * motion[axis]
                    flux.append(term + pressure if other == axis else term)
                flux.append((parts[4] + pressure) * motion[axis])
                for v in range(5):
                    if axis == 0:
                        ftmp[0, v, rows] = flux[v]
                    elif axis == 2:
                        ftmp[1, v, rows] = flux[v]
                    else:
                        total = weights[0] * flux[v]
                        for shift in range(1, 4):
                            total += weights[shift] * pltpu.roll(flux[v], 4 * shift, axis=0)
                        res[c, v, rows] = total

    def slopes_of(c):
        for v in range(5):
            terms = [ftmp[0, v, 16 * i : 16 * i + 16] for i in range(4)]
            for a in range(4):
                total = res[c, v, 16 * a : 16 * a + 16]
                for i in range(4):
                    total += derivative[a][i] * terms[i]
                res[c, v, 16 * a : 16 * a + 16] = total
        for v in range(5):
            terms = [ftmp[1, v, pl.ds(k, 16, 4)] for k in range(4)]
            for a in range(4):
                total = res[c, v, pl.ds(a, 16, 4)]
                for k in range(4):
                    total += derivative[a][k] * terms[k]
                res[c, v, pl.ds(a, 16, 4)] = total

    def own_fluxes_of(c):
        for f in range(6):
            flux, speed = axis_flux(split(tr[f, c]), SIDE[f], 2.0 * (f % 2) - 1.0)
            for v in range(5):
                own[f, c, 16 * v : 16 * v + 16] = flux[v]
            spd[f, c] = speed

    def outgoing(p):
        index = send_ref[pl.ds(p, 1), :]
        tile = wide(jnp.right_shift(index, 7))
        place = wide(jnp.bitwise_and(index, 127))
        value = rest
        for f in range(6):
            for c in range(TILES):
                value = jnp.where(tile == f * TILES + c, lanes_of(tr[f, c], place), value)
        snd[p] = value

    def send_step(c, carry):
        p = lax.rem(4 - c, 4)
        outgoing(p)
        outgoing(p + 4)
        return carry

    small[0].wait()
    lax.fori_loop(0, TILES, send_step, 0)
    pl.semaphore_wait(barrier, 8)
    for p in (4, 0):
        trace_copy(p).start()

    for n in (1, 2, 3):
        small[n].wait()
    pad[...] = jnp.full((8, 128), 3072, jnp.int32)
    pad[0:5, 0:40] = mortar_ref[...]
    pad[5:6, 0:40] = dir_ref[...]
    pad[6:8, 0:32] = return_ref[...]
    packed = pad[...]
    by40 = pltpu.roll(packed, 40, axis=1)
    by80 = pltpu.roll(packed, 80, axis=1)
    entry = [
        jnp.where(
            lane1 < 40,
            packed[0:1],
            jnp.where(lane1 < 80, by40[1:2], jnp.where(lane1 < 120, by80[2:3], 3072)),
        ),
        jnp.where(lane1 < 40, packed[3:4], jnp.where(lane1 < 80, by40[4:5], 3072)),
    ]
    direction = [
        jnp.where(lane1 < 40, packed[5:6], jnp.where(lane1 < 80, by40[5:6], by80[5:6])),
        jnp.where(lane1 < 40, packed[5:6], by40[5:6]),
    ]
    by32 = pltpu.roll(packed, 32, axis=1)
    by64 = pltpu.roll(packed, 64, axis=1)
    by96 = pltpu.roll(packed, 96, axis=1)
    leaving = jnp.where(
        lane < 32, packed, jnp.where(lane < 64, by32, jnp.where(lane < 96, by64, by96))
    )[6:8]

    for m in range(2):
        tile, place = placed(entry[m])
        tile, place = wide(tile), wide(place)
        value = rest
        for f in range(4):
            for c in range(TILES):
                value = jnp.where(tile == f * TILES + c, lanes_of(tr[f, c], place), value)
        mor[m] = value

    for p in (7, 3, 6, 2, 5, 1):
        trace_copy(p).start()
    small[4].wait()

    def local_step(c, carry):
        fluxes_of(c)
        slopes_of(c)
        own_fluxes_of(c)
        for v in range(5):
            lift_j[c, v] = jnp.zeros((64, 128), jnp.float32)
            lift_k[c, v] = jnp.zeros((64, 128), jnp.float32)
        span = pl.ds(pl.multiple_of(128 * c, 128), 128)
        for f in range(6):
            tile, place = placed(partner_ref[f : f + 1, span])
            tile, place = wide(tile), wide(place)
            value = rest
            for t in range(TILES):
                value = jnp.where(
                    tile == (f ^ 1) * TILES + t, lanes_of(tr[f ^ 1, t], place), value
                )
            acc[f, c] = value
        return carry

    lax.fori_loop(0, TILES, local_step, 0)

    trace_copy(0).wait_recv()
    trace_copy(4).wait_recv()
    small[7].wait()
    states = []
    for m in range(2):
        tile, place = placed(entry[m])
        tile, place = wide(tile), wide(place)
        value = mor[m]
        for p in (0, 4):
            value = jnp.where(tile == 24 + p, lanes_of(rcv[p], place), value)
        states.append(value)
    lane80 = wide(lane1)
    big = jnp.where(
        lane80 < 40,
        states[0],
        jnp.where(
            lane80 < 80,
            pltpu.roll(states[0], 40, axis=1),
            pltpu.roll(states[0], 80, axis=1),
        ),
    )
    near = product(matrix_ref[0:320], big)
    nears = [
        jnp.where(lane80 < 80, near[0:80], near[80:160]),
        jnp.where(lane80 < 40, near[160:240], near[240:320]),
    ]
    stars = []
    for m in range(2):
        normal = [
            wide(
                jnp.where(direction[m] == 2 * axis + 1, 1.0, 0.0)
                - jnp.where(direction[m] == 2 * axis, 1.0, 0.0),
                16,
            )
            for axis in range(3)
        ]
        inside, outside = split(nears[m]), split(states[m])
        inside_flux, inside_speed = normal_flux(inside, normal)
        outside_flux, outside_speed = normal_flux(outside, normal)
        half = 0.5 * jnp.maximum(inside_speed, outside_speed)
        stars.append(
            jnp.concatenate(
                [
                    0.5 * (inside_flux[v] + outside_flux[v]) - half * (outside[v] - inside[v])
                    for v in range(5)
                ],
                axis=0,
            )
        )
    home_a = product(matrix_ref[320:480], stars[0])
    home_b = product(matrix_ref[480:640], stars[1])
    together = (
        pltpu.roll(home_a[0:80], 88, axis=1)
        + pltpu.roll(home_a[80:160], 48, axis=1)
        + home_b[0:80]
        + pltpu.roll(home_b[80:160], 88, axis=1)
    )
    tab[0] = jnp.where(lane80 < 40, together, -stars[0])
    tab[1] = -stars[1]

    def return_copy(side):
        step = 1 - 2 * side
        return pltpu.make_async_remote_copy(
            src_ref=rsnd.at[side],
            dst_ref=rrcv.at[side],
            send_sem=rsend_sem.at[side],
            recv_sem=rrecv_sem.at[side],
            device_id=(lax.rem(me + step + count, count),),
            device_id_type=MESH,
        )

    quarter = jnp.right_shift(lane, 5)
    for side in range(2):
        index = wide(leaving[side : side + 1], 8)
        first = index < 120
        named = index < 200
        place = jnp.bitwise_and(jnp.where(first, index, index - 120), 127)
        for k in range(3):
            value = jnp.zeros((8, 128), jnp.float32)
            for b in range(4):
                g = 4 * k + b
                if g < 10:
                    rows = slice(8 * g, 8 * g + 8)
                    found = jnp.where(
                        first, lanes_of(tab[0, rows], place), lanes_of(tab[1, rows], place)
                    )
                    value = jnp.where((quarter == b) & named, found, value)
            rsnd[side, 8 * k : 8 * k + 8] = value
        return_copy(side).start()

    small[5].wait()

    def hang_step(c, carry):
        span = pl.ds(pl.multiple_of(128 * c, 128), 128)
        for f in range(4):
            index = wide(source_ref[f : f + 1, span])
            first = index < 120
            place = jnp.bitwise_and(jnp.where(first, index, index - 120), 127)
            found = jnp.where(first, lanes_of(tab[0], place), lanes_of(tab[1], place))
            hang[f, c] = jnp.where(index < 200, found - own[f, c], 0.0)
        return carry

    lax.fori_loop(0, TILES, hang_step, 0)

    def arrive_step(k, carry):
        p = lax.rem(4 - k, 4)

        @pl.when(k >= 1)
        def _():
            trace_copy(p).wait_recv()
            trace_copy(p + 4).wait_recv()

        for c in range(TILES):
            for f in range(6):
                tile, place = placed(partner_ref[f : f + 1, 128 * c : 128 * c + 128])
                tile, place = wide(tile), wide(place)
                value = acc[f, c]
                for q in (p, p + 4):
                    value = jnp.where(tile == 24 + q, lanes_of(rcv[q], place), value)
                acc[f, c] = value
        return carry

    lax.fori_loop(0, 4, arrive_step, 0)
    small[6].wait()

    for c in range(TILES):
        span = slice(128 * c, 128 * c + 128)
        ends = [[None] * 5, [None] * 5]
        for f in range(6):
            here, there = tr[f, c], acc[f, c]
            inside, outside = split(here), split(there)
            flux, speed = axis_flux(outside, SIDE[f], 2.0 * (f % 2) - 1.0)
            half = 0.5 * jnp.maximum(spd[f, c], speed)
            jumps = [
                0.5 * (flux[v] - own[f, c, 16 * v : 16 * v + 16]) - half * (outside[v] - inside[v])
                for v in range(5)
            ]
            if f < 4:
                plain = wide(source_ref[f : f + 1, span], 16) == 200
                for v in range(5):
                    jumps[v] = jnp.where(plain, jumps[v], hang[f, c, 16 * v : 16 * v + 16])
            for v in range(5):
                if f < 2:
                    ends[f][v] = jumps[v]
                elif f < 4:
                    for i in range(4):
                        at = 16 * i + 12 * (f - 2)
                        lift_j[c, v, at : at + 4] = jumps[v][4 * i : 4 * i + 4]
                else:
                    lift_k[c, v, pl.ds(3 * (f - 4), 16, 4)] = jumps[v]
        for v in range(5):
            for i in range(4):
                rows = slice(16 * i, 16 * i + 16)
                lift = lift_j[c, v, rows] + lift_k[c, v, rows]
                if i in (0, 3):
                    lift += ends[i // 3][v]
                res[c, v, rows] += 6.0 * lift

    return_copy(0).wait_recv()
    return_copy(1).wait_recv()
    for p in range(8):
        trace_copy(p).wait_send()
    for side in range(2):
        return_copy(side).wait_send()


def close_kernel(
    res,
    own,
    rrcv,
    source_ref,
    levels_ref,
    step_ref,
    out_hbm,
    done,
    lift_j,
    out_sem,
):
    def wide(row, rows):
        return jnp.broadcast_to(row, (rows, 128))

    copies = []
    for v in range(5):
        lift_j[v] = jnp.zeros((64, 128), jnp.float32)
    for c in range(TILES):
        span = slice(128 * c, 128 * c + 128)
        ends = [[None] * 5, [None] * 5]
        for f in range(4):
            index = wide(source_ref[f : f + 1, span], 8)
            near_side, named = index < 233, index > 200
            back = jnp.bitwise_and(jnp.where(near_side, index - 201, index - 233), 31)
            backs = [back + 32 * b for b in range(4)]
            for v in range(5):
                pieces = []
                for g in (2 * v, 2 * v + 1):
                    packs = slice(8 * (g // 4), 8 * (g // 4) + 8)
                    far = backs[g % 4]
                    came = jnp.where(
                        near_side,
                        lanes_of(rrcv[0, packs], far),
                        lanes_of(rrcv[1, packs], far),
                    )
                    pieces.append(
                        jnp.where(named, came - own[f, c, 8 * g : 8 * g + 8], 0.0)
                    )
                if f < 2:
                    ends[f][v] = jnp.concatenate(pieces, axis=0)
                else:
                    for i in range(4):
                        at = 16 * i + 12 * (f - 2)
                        half_rows = slice(4 * (i % 2), 4 * (i % 2) + 4)
                        lift_j[v, at : at + 4] = pieces[i // 2][half_rows]
        scale = -step_ref[0] * jnp.exp2(levels_ref[0:1, span].astype(jnp.float32) + 1.0)
        for v in range(5):
            for i in range(4):
                rows = slice(16 * i, 16 * i + 16)
                lift = lift_j[v, rows]
                if i in (0, 3):
                    lift += ends[i // 3][v]
                done[c, v, rows] = wide(scale, 16) * (res[c, v, rows] + 6.0 * lift)
        copies.append(
            pltpu.make_async_copy(done.at[c], out_hbm.at[:, :, span], out_sem.at[c])
        )
        copies[c].start()
    for copy in copies:
        copy.wait()


def body(
    state, step_size, levels, send_faces, partner, mortar_in, mortar_dir, return_faces, flux_source
):


    count = lax.axis_size("dev")
    vmem = pl.BlockSpec(memory_space=pltpu.VMEM)
    f32 = jnp.float32
    kept = (
        pltpu.VMEM((TILES, 5, 64, 128), f32),
        pltpu.VMEM((6, TILES, 80, 128), f32),
        pltpu.VMEM((2, 24, 128), f32),
        pltpu.VMEM((6, 512), jnp.int32),
        pltpu.VMEM((1, 512), jnp.int32),
    )
    parts = pl.pallas_call(
        functools.partial(kernel, count),
        out_shape=kept,
        in_specs=[pl.BlockSpec(memory_space=pltpu.HBM)] * 9,
        out_specs=(vmem,) * 5,
        scratch_shapes=[
            pltpu.VMEM((8, 128), jnp.int32),
            pltpu.VMEM((6, 512), jnp.int32),
            pltpu.VMEM((5, 40), jnp.int32),
            pltpu.VMEM((1, 40), jnp.int32),
            pltpu.VMEM((2, 32), jnp.int32),
            pltpu.VMEM((640, 240), jnp.bfloat16),
            pltpu.VMEM((TILES, 5, 64, 128), f32),
            pltpu.VMEM((6, TILES, 80, 128), f32),
            pltpu.VMEM((8, 80, 128), f32),
            pltpu.VMEM((8, 80, 128), f32),
            pltpu.VMEM((6, TILES, 80, 128), f32),
            pltpu.VMEM((6, TILES, 16, 128), f32),
            pltpu.VMEM((2, 5, 64, 128), f32),
            pltpu.VMEM((2, 80, 128), f32),
            pltpu.VMEM((2, 80, 128), f32),
            pltpu.VMEM((2, 24, 128), f32),
            pltpu.VMEM((8, 128), jnp.int32),
            pltpu.VMEM((4, TILES, 80, 128), f32),
            pltpu.VMEM((TILES, 5, 64, 128), f32),
            pltpu.VMEM((TILES, 5, 64, 128), f32),
            pltpu.SemaphoreType.DMA((TILES,)),
            pltpu.SemaphoreType.DMA((8,)),
            pltpu.SemaphoreType.DMA((8,)),
            pltpu.SemaphoreType.DMA((8,)),
            pltpu.SemaphoreType.DMA((2,)),
            pltpu.SemaphoreType.DMA((2,)),
        ],
        compiler_params=pltpu.CompilerParams(
            collective_id=0, has_side_effects=True, vmem_limit_bytes=24 * 1024 * 1024
        ),
        name="section",
    )(
        *(
            pltpu.with_memory_space_constraint(array, pltpu.HBM)
            for array in (
                state,
                levels.reshape(1, -1),
                send_faces,
                partner,
                mortar_in,
                mortar_dir.reshape(1, -1),
                return_faces,
                flux_source,
                jnp.asarray(mortar_matrices()),
            )
        )
    )
    return pl.pallas_call(
        close_kernel,
        out_shape=jax.ShapeDtypeStruct(state.shape, f32),
        in_specs=[vmem] * 5 + [pl.BlockSpec(memory_space=pltpu.SMEM)],
        out_specs=pl.BlockSpec(memory_space=pltpu.HBM),
        scratch_shapes=[
            pltpu.VMEM((TILES, 5, 64, 128), f32),
            pltpu.VMEM((5, 64, 128), f32),
            pltpu.SemaphoreType.DMA((TILES,)),
        ],
        compiler_params=pltpu.CompilerParams(vmem_limit_bytes=8 * 1024 * 1024),
        name="close",
    )(*(pltpu.with_memory_space_constraint(part, pltpu.VMEM) for part in parts), step_size)


def solution(mesh):
    placed = (
        P(None, None, "dev"),
        P(),
        P("dev"),
        P("dev", None),
        P(None, "dev"),
        P(None, "dev"),
        P("dev"),
        P("dev", None),
        P(None, "dev"),
    )
    return jax.shard_map(
        body, mesh=mesh, in_specs=placed, out_specs=P(None, None, "dev"), check_vma=False
    )
```
